512 devices in a mesh: slab: 4 (over y_hi, core), wide: 128 (over y_lo, z, x).
Axes of the slice: x: 4, y: 4 (y_hi: 2, y_lo: 2; y = y_hi * 2 + y_lo), z: 16, core: 2. Of those that a mesh axis runs over, the one named last changes fastest.
Arguments:
- spectrum: float32 [1152, 512, 128], P('wide', 'slab'), may hold values from 0 to 1
- sea_mask: int32 [512, 128], P('slab'), may hold values 0 or 1
- courant: float32 [32], replicated, may hold values from 0.05 to 0.7
- slot_owner: int32 [1152], replicated, may hold values from 0 to 1151, each once
- coupling: bfloat16 [1152, 1152], replicated, may hold values from -0.1875 to 0.1875
Outputs:
- evolved: float32 [1152, 512, 128], P('wide', 'slab')
The draws below stay inside these ranges and needn't reach their ends.
Inputs may be any that keep to these rules, and one draw needn't show every extreme that they name: `slot_owner`: each component occurs in exactly one slot; component f * 36 + d has direction d and frequency f. `sea_mask`: 1 marks a sea point.
All inputs are finite; a program needn't handle non-finite values. No bound on the sum of `sea_mask` on one device may be relied on, other than what follows from the above.
Results may differ from the reference program's by a relative error of at most 0.0015.
Values sent between devices are 32-bit elements; how exact they have to be, the bound alone decides.
A program may use at most 64 MiB of HBM per device.

```python
import math
import jax
import jax.numpy as jnp
from jax import lax

ND = 36
NF = 32
STEPS = 2
NLON = 128
K = 1152
NLAT = 512
N_SLAB = 4


def plant(drawn, key, least, largest):
    longest = drawn.shape.index(max(drawn.shape))
    spots = []
    for shift in (0, 1):
        where = [jax.random.randint(jax.random.fold_in(key, axis), (), 0, length) for axis, length in enumerate(drawn.shape)]
        where[longest] = (where[longest] + shift) % drawn.shape[longest]
        spots.append(tuple(where))
    return drawn.at[spots[0]].set(least).at[spots[1]].set(largest)


def steps_of(rng, extent, shards, least, largest):
    level, own = 1.0, jax.random.fold_in(rng, 6)
    for position, parts in shards:
        steps = jnp.exp(jax.random.uniform(jax.random.fold_in(own, position), (parts,), jnp.float32, least / len(shards), largest / len(shards)))
        level = level * jnp.repeat(steps, extent[position] // parts).reshape([-1 if axis == position else 1 for axis in range(len(extent))])
    return level


def gaussian(rng, shape, scale, reach, held_as=jnp.bfloat16):
    drawn = jax.random.normal(rng, shape, jnp.float32) * scale
    return jnp.minimum(jnp.maximum(drawn, -reach), reach).astype(held_as)


def setup_inputs(seed: int = 0) -> dict:
    streams_of = jax.random.split(jax.random.key(seed), 6)
    spectrum = jnp.clip(1.0 * jax.random.uniform(streams_of[0], (K, NLAT, NLON), jnp.float32) ** steps_of(streams_of[0], (K, NLAT, NLON), ((0, 128), (1, 4)), -0.2, 0.2), 0.0, 1.0)
    sea_mask = plant((jax.random.randint(streams_of[1], (NLAT, NLON), 0, 4) < 3).astype(jnp.int32), jax.random.fold_in(streams_of[1], 1), 0, 1)
    courant = jnp.clip(jnp.exp(jax.random.uniform(streams_of[2], (NF,), jnp.float32, math.log(0.05), math.log(0.7))), 0.05, 0.7)
    slot_owner = jax.random.permutation(streams_of[3], K).astype(jnp.int32)
    coupling = gaussian(streams_of[4], (K, K), K ** -0.5, 0.1875)
    return dict(spectrum=spectrum, sea_mask=sea_mask, courant=courant, slot_owner=slot_owner, coupling=coupling)


time_step = 0.5


def velocities(slot_owner, courant):
    band_count = courant.shape[0]
    heading = slot_owner % ND
    freq_band = slot_owner // ND
    picked = freq_band[:, None] == jnp.arange(band_count, dtype=jnp.int32)[None, :]
    wave_speed = jnp.sum(jnp.where(picked, courant[None, :], 0.0), axis=1)
    wave_angle = heading.astype(jnp.float32) * (2.0 * math.pi / ND)
    return wave_speed * jnp.cos(wave_angle), wave_speed * jnp.sin(wave_angle)


def advect(energy, padded, east_speed, north_speed):
    east_speed = east_speed[:, None, None]
    north_speed = north_speed[:, None, None]
    remain = 1.0 - jnp.abs(east_speed) - jnp.abs(north_speed)
    west_side = jnp.roll(energy, 1, axis=2)
    east_side = jnp.roll(energy, -1, axis=2)
    south_side = padded[:, :-2, :]
    north_side = padded[:, 2:, :]
    result = remain * energy + jnp.maximum(east_speed, 0.0) * west_side
    result = result + jnp.maximum(-east_speed, 0.0) * east_side
    result = result + jnp.maximum(north_speed, 0.0) * south_side
    return result + jnp.maximum(-north_speed, 0.0) * north_side


def interact(moved, slot_table):
    slot_count = moved.shape[0]
    flattened = moved.reshape(slot_count, -1)
    rounded = flattened.astype(jnp.bfloat16)
    square = (flattened * flattened).astype(jnp.bfloat16)
    gain_term = flattened * jnp.dot(slot_table, rounded, preferred_element_type=jnp.float32)
    loss_term = lax.dot_general(slot_table, square, (((0,), (0,)), ((), ())), preferred_element_type=jnp.float32)
    updated = jnp.maximum(flattened + time_step * (gain_term - loss_term), 0.0)
    return updated.reshape(moved.shape)


def reference(spectrum, sea_mask, courant, slot_owner, coupling):
    sea_float = sea_mask.astype(jnp.float32)
    east_speed, north_speed = velocities(slot_owner, courant)
    slot_table = jnp.take(jnp.take(coupling, slot_owner, axis=0), slot_owner, axis=1)
    energy = spectrum * sea_float[None]
    block_rows = NLAT // N_SLAB
    for repeat in range(STEPS):
        padded = jnp.pad(energy, ((0, 0), (1, 1), (0, 0)))
        moved = advect(energy, padded, east_speed, north_speed)

        def one_block(block_index):
            segment = lax.dynamic_slice_in_dim(moved, block_index * block_rows, block_rows, 1)
            return interact(segment, slot_table)

        pieces = lax.map(one_block, jnp.arange(N_SLAB, dtype=jnp.int32))
        energy = jnp.moveaxis(pieces, 0, 1).reshape(moved.shape) * sea_float[None]
    return energy
```

```python
import math

import jax
import jax.numpy as jnp
from jax import lax
from jax.experimental import pallas as pl
from jax.experimental.pallas import tpu as pltpu
from jax.sharding import PartitionSpec as P

ND = 36
STEPS = 2


time_step = 0.5


WIDE = 128
OWN = 9
PAD = 16


def peer_of(me, step):
    y, z, x = me // 64, (me // 4) % 16, me % 4
    turn, plane = step % 16, step // 16
    half = (turn + 1) // 2
    dz = jnp.where(turn % 2 == 1, half, 16 - half)
    return ((y + plane // 4) % 2) * 64 + ((z + dz) % 16) * 4 + (x + plane % 4) % 4


def transpose_kernel(x_ref, o_ref, outbox, inbox, send_sem, recv_sem):
    me = lax.axis_index("wide")
    barrier = pltpu.get_barrier_semaphore()

    def greet(step, carry):
        pl.semaphore_signal(
            barrier, inc=1, device_id={"wide": peer_of(me, step)}, device_id_type=pl.DeviceIdType.MESH
        )
        return carry

    lax.fori_loop(1, WIDE, greet, 0)
    for j in range(OWN):
        outbox[pl.ds(j, WIDE, stride=PAD), :] = x_ref[j]
    pl.semaphore_wait(barrier, WIDE - 1)
    mine = pl.ds(pl.multiple_of(me * PAD, PAD), OWN)

    def send(step, carry):
        peer = peer_of(me, step)
        pltpu.make_async_remote_copy(
            src_ref=outbox.at[pl.ds(pl.multiple_of(peer * PAD, PAD), OWN)],
            dst_ref=inbox.at[mine],
            send_sem=send_sem,
            recv_sem=recv_sem,
            device_id={"wide": peer},
            device_id_type=pl.DeviceIdType.MESH,
        ).start()
        return carry

    lax.fori_loop(1, WIDE, send, 0)
    pltpu.make_async_copy(outbox.at[mine], inbox.at[mine], recv_sem).start()
    pltpu.make_async_copy(x_ref, x_ref, recv_sem).wait()
    for j in range(OWN):
        o_ref[j] = inbox[pl.ds(j, WIDE, stride=PAD), :]
    most = x_ref.at[pl.ds(0, OWN - 1)]
    pltpu.make_async_copy(most, most, send_sem).wait()
    rest = x_ref.at[0, pl.ds(0, WIDE - OWN)]
    pltpu.make_async_copy(rest, rest, send_sem).wait()


def transpose_over_wide(value, collective_id):
    return pl.pallas_call(
        transpose_kernel,
        out_shape=jax.ShapeDtypeStruct((OWN, WIDE, 128), jnp.float32),
        in_specs=[pl.BlockSpec(memory_space=pltpu.VMEM)],
        out_specs=pl.BlockSpec(memory_space=pltpu.VMEM),
        scratch_shapes=[
            pltpu.VMEM((WIDE * PAD, 128), jnp.float32),
            pltpu.VMEM((WIDE * PAD, 128), jnp.float32),
            pltpu.SemaphoreType.DMA,
            pltpu.SemaphoreType.DMA,
        ],
        compiler_params=pltpu.CompilerParams(
            collective_id=collective_id, has_side_effects=True, vmem_limit_bytes=16 << 20
        ),
    )(value)


def with_halo(value, sides, width):
    edges = {}
    for axis, dim in sides:
        count, length = (lax.axis_size(axis), value.shape[dim])
        up = [(i, (i + 1) % count) for i in range(count - 1)]
        last = lax.slice_in_dim(value, length - width, length, axis=dim)
        first = lax.slice_in_dim(value, 0, width, axis=dim)
        edges[dim] = (
            lax.ppermute(last, axis, up),
            lax.ppermute(first, axis, [(b, a) for a, b in up]),
        )
    done = []
    for _, dim in sides:
        low, high = edges[dim]
        around = [(width, width) if d in done else (0, 0) for d in range(value.ndim)]
        value = jnp.concatenate([jnp.pad(low, around), value, jnp.pad(high, around)], axis=dim)
        done.append(dim)
    return value


def velocities(slot_owner, courant):
    band_count = courant.shape[0]
    heading = slot_owner % ND
    freq_band = slot_owner // ND
    picked = freq_band[:, None] == jnp.arange(band_count, dtype=jnp.int32)[None, :]
    wave_speed = jnp.sum(jnp.where(picked, courant[None, :], 0.0), axis=1)
    wave_angle = heading.astype(jnp.float32) * (2.0 * math.pi / ND)
    return (wave_speed * jnp.cos(wave_angle), wave_speed * jnp.sin(wave_angle))


def combine_sides(energy, west_side, east_side, south_side, north_side, east_speed, north_speed):
    east_speed = east_speed[:, None, None]
    north_speed = north_speed[:, None, None]
    remain = 1.0 - jnp.abs(east_speed) - jnp.abs(north_speed)
    result = remain * energy + jnp.maximum(east_speed, 0.0) * west_side
    result = result + jnp.maximum(-east_speed, 0.0) * east_side
    result = result + jnp.maximum(north_speed, 0.0) * south_side
    return result + jnp.maximum(-north_speed, 0.0) * north_side


def advect(energy, padded, east_speed, north_speed):
    west_side = jnp.roll(energy, 1, axis=2)
    east_side = jnp.roll(energy, -1, axis=2)
    return combine_sides(
        energy, west_side, east_side, padded[:, :-2, :], padded[:, 2:, :], east_speed, north_speed
    )


def interact(moved, slot_table):
    slot_count = moved.shape[0]
    flattened = moved.reshape(slot_count, -1)
    rounded = flattened.astype(jnp.bfloat16)
    square = (flattened * flattened).astype(jnp.bfloat16)
    gain_term = flattened * jnp.dot(slot_table, rounded, preferred_element_type=jnp.float32)
    loss_term = lax.dot_general(
        slot_table, square, (((0,), (0,)), ((), ())), preferred_element_type=jnp.float32
    )
    updated = jnp.maximum(flattened + time_step * (gain_term - loss_term), 0.0)
    return updated.reshape(moved.shape)


def body(spectrum, sea_mask, courant, slot_owner, coupling):
    wide_index = lax.axis_index("wide")
    sea_float = sea_mask.astype(jnp.float32)
    slot_owner = slot_owner.reshape(WIDE, OWN).T.reshape(-1)
    slot_table = jnp.take(jnp.take(coupling, slot_owner, axis=0), slot_owner, axis=1)
    local_sea = lax.dynamic_slice_in_dim(sea_float, wide_index, 1, 0)
    east_speed, north_speed = velocities(slot_owner, courant)
    energy = transpose_over_wide(spectrum * sea_float[None], 0).reshape(OWN * WIDE, 1, 128)
    for repeat in range(STEPS):
        padded = with_halo(energy, ((("slab", "wide"), 1),), 1)
        moved = advect(energy, padded, east_speed, north_speed)
        energy = interact(moved, slot_table) * local_sea[None]
    return transpose_over_wide(energy.reshape(OWN, WIDE, 128), 1)


def solution(mesh):
    return jax.shard_map(
        body,
        mesh=mesh,
        in_specs=(P("wide", "slab", None), P("slab", None), P(), P(), P()),
        out_specs=P("wide", "slab", None),
        check_vma=False,
    )
```

```python
import math

import jax
import jax.numpy as jnp
from jax import lax
from jax.experimental import pallas as pl
from jax.experimental.pallas import tpu as pltpu
from jax.sharding import PartitionSpec as P

ND = 36
WIDE = 128
OWN = 9
PAD = 16
SLOTS = OWN * WIDE
ROWS = 128
HOLD = 144
TOP = 8
TILE = 16
GROUP = 144
HALF = 72
MESH = pl.DeviceIdType.MESH

time_step = 0.5


def place(me):
    return me // 64, (me // 4) % 16, me % 4


def tile_of(y, x):
    return jnp.where(y == 0, x, 7 - x)


def device_of(z, q):
    y = q // 4
    return y * 64 + z * 4 + jnp.where(y == 0, q, 7 - q)


def peer_of(me, step):
    y, z, x = place(me)
    turn, plane = step % 16, step // 16
    half = (turn + 1) // 2
    dz = jnp.where(turn % 2 == 1, half, 16 - half)
    return ((y + plane // 4) % 2) * 64 + ((z + dz) % 16) * 4 + (x + plane % 4) % 4


def swap_blocks(parts, block):
    parts = list(parts)
    for bit in (4, 2, 1):
        high = (block & bit) != 0
        for a in range(8):
            if a & bit:
                continue
            first, second = parts[a], parts[a + bit]
            parts[a] = jnp.where(high, pltpu.roll(second, TILE * bit, 1), first)
            parts[a + bit] = jnp.where(high, second, pltpu.roll(first, 128 - TILE * bit, 1))
    return parts


def kernel(
    spectrum,
    sea_mask,
    own_speed,
    slot_speed,
    owner,
    coupling,
    out,
    plane,
    table_in,
    outbox,
    inbox,
    outbox2,
    inbox2,
    rim_out,
    rim_in,
    picker,
    picker_t,
    half_table,
    table,
    table_t,
    owner_wide,
    east_wide,
    north_wide,
    moved,
    rounded,
    square,
    energy,
    row_out,
    row_in,
    col_out,
    col_in,
    load_sem,
    table_sem,
    send_sem,
    recv_sem,
    send_sem2,
    recv_sem2,
    rim_send,
    rim_recv,
    edge_send,
    edge_recv,
):
    slab = lax.axis_index("slab")
    me = lax.axis_index("wide")
    y, z, x = place(me)
    q = tile_of(y, x)
    spot = z * 8 + q
    up_slab, down_slab = (slab + 1) % 4, (slab + 3) % 4
    north_id = {
        "slab": jnp.where(z == 15, up_slab, slab),
        "wide": y * 64 + ((z + 1) % 16) * 4 + x,
    }
    south_id = {
        "slab": jnp.where(z == 0, down_slab, slab),
        "wide": y * 64 + ((z + 15) % 16) * 4 + x,
    }
    east_id = {"slab": slab, "wide": device_of(z, (q + 1) % 8)}
    west_id = {"slab": slab, "wide": device_of(z, (q + 7) % 8)}

    loads = pltpu.make_async_copy(spectrum, plane.at[:, pl.ds(TOP, ROWS)], load_sem)
    loads.start()
    table_load = pltpu.make_async_copy(coupling, table_in, table_sem)
    table_load.start()

    barrier = pltpu.get_barrier_semaphore()
    for there in (
        {"slab": up_slab, "wide": me},
        {"slab": down_slab, "wide": me},
        north_id,
        south_id,
    ):
        pl.semaphore_signal(barrier, inc=1, device_id=there, device_id_type=MESH)

    def greet(step, carry):
        pl.semaphore_signal(
            barrier, inc=1, device_id={"slab": slab, "wide": peer_of(me, step)}, device_id_type=MESH
        )
        return carry

    lax.fori_loop(1, WIDE, greet, 0)

    lane = lax.broadcasted_iota(jnp.int32, (8, 128), 1)
    block = lane // TILE

    loads.wait()
    sea = sea_mask[...].astype(jnp.float32)
    for j in range(OWN):
        plane[j, pl.ds(TOP, ROWS), :] = plane[j, pl.ds(TOP, ROWS), :] * sea
        plane[j, pl.ds(TOP - 8, 8), :] = jnp.zeros((8, 128), jnp.float32)
        plane[j, pl.ds(TOP + ROWS, 8), :] = jnp.zeros((8, 128), jnp.float32)
        rim_out[0, pl.ds(j, 1), :] = own_speed[3 * OWN + j] * plane[j, pl.ds(TOP + ROWS - 1, 1), :]
        rim_out[1, pl.ds(j, 1), :] = own_speed[4 * OWN + j] * plane[j, pl.ds(TOP, 1), :]

    def propagate(j, carry):
        remain = own_speed[j]
        east, west = own_speed[OWN + j], own_speed[2 * OWN + j]
        north, south = own_speed[3 * OWN + j], own_speed[4 * OWN + j]
        for h in range(2):
            parts = []
            for k in range(8):
                start = TOP + 8 * h + k
                here = plane[j, pl.ds(start, 8, stride=16), :]
                part = remain * here + east * pltpu.roll(here, 1, 1)
                part = part + west * pltpu.roll(here, 127, 1)
                part = part + north * plane[j, pl.ds(start - 1, 8, stride=16), :]
                parts.append(part + south * plane[j, pl.ds(start + 1, 8, stride=16), :])
            for k, part in enumerate(swap_blocks(parts, block)):
                outbox[pl.ds(h * 128 + k * PAD + j, 8, stride=256), :] = part
        return carry

    lax.fori_loop(0, OWN, propagate, 0)

    pl.semaphore_wait(barrier, WIDE - 1 + 4)

    rims = []
    for side, there in ((0, up_slab), (1, down_slab)):
        rims.append(
            pltpu.make_async_remote_copy(
                src_ref=rim_out.at[side, pl.ds(0, OWN)],
                dst_ref=rim_in.at[side, pl.ds(0, OWN)],
                send_sem=rim_send.at[side],
                recv_sem=rim_recv.at[side],
                device_id={"slab": there, "wide": me},
                device_id_type=MESH,
            )
        )
        rims[-1].start()
    for rim in rims:
        rim.wait()
    lane9 = lax.broadcasted_iota(jnp.int32, (OWN, 128), 1)
    below = jnp.where(slab > 0, 1.0, 0.0) * rim_in[0, pl.ds(0, OWN), :]
    above = jnp.where(slab < 3, 1.0, 0.0) * rim_in[1, pl.ds(0, OWN), :]
    for k in range(8):
        low = pltpu.roll(below, (128 - TILE * k) % 128, 1) if k else below
        rows = pl.ds(k * PAD, OWN)
        outbox[rows, :] = outbox[rows, :] + jnp.where(lane9 < TILE, low, 0.0)
        high = pltpu.roll(above, 112 - TILE * k, 1) if k < 7 else above
        rows = pl.ds((15 * 8 + k) * PAD, OWN)
        outbox[rows, :] = outbox[rows, :] + jnp.where(lane9 >= 112, high, 0.0)

    mine = pl.ds(pl.multiple_of(me * PAD, PAD), OWN)
    my_tile = pl.ds(pl.multiple_of(spot * PAD, PAD), OWN)

    def send(step, carry):
        peer = peer_of(me, step)
        py, pz, px = place(peer)
        row = (pz * 8 + tile_of(py, px)) * PAD
        pltpu.make_async_remote_copy(
            src_ref=outbox.at[pl.ds(pl.multiple_of(row, PAD), OWN)],
            dst_ref=inbox.at[mine],
            send_sem=send_sem,
            recv_sem=recv_sem,
            device_id={"slab": slab, "wide": peer},
            device_id_type=MESH,
        ).start()
        return carry

    lax.fori_loop(1, WIDE, send, 0)
    pltpu.make_async_copy(outbox.at[my_tile], inbox.at[mine], recv_sem).start()

    for j in range(OWN):
        rows = pl.ds(j * WIDE, WIDE)
        owner_wide[rows, :] = jnp.broadcast_to(owner[pl.ds(j, 1), :], (128, 128)).T
        east_wide[rows, :] = jnp.broadcast_to(slot_speed[pl.ds(j, 1), :], (128, 128)).T
        north_wide[rows, :] = jnp.broadcast_to(slot_speed[pl.ds(OWN + j, 1), :], (128, 128)).T

    lanes = lax.broadcasted_iota(jnp.int32, (128, 128), 1).astype(jnp.float32)
    sublanes = lax.broadcasted_iota(jnp.int32, (128, 128), 0).astype(jnp.float32)

    def pick(i, carry):
        rows = pl.ds(pl.multiple_of(i * 128, 128), 128)
        base = (i * 128).astype(jnp.float32)
        for j in range(OWN):
            columns = pl.ds(j * 128, 128)
            hit = owner_wide[rows, :] == lanes + 128.0 * j
            picker[rows, columns] = jnp.where(hit, 1.0, 0.0).astype(jnp.bfloat16)
            hit = owner[pl.ds(j, 1), :] == sublanes + base
            picker_t[rows, columns] = jnp.where(hit, 1.0, 0.0).astype(jnp.bfloat16)
        return carry

    lax.fori_loop(0, OWN, pick, 0)
    table_load.wait()

    def rows_picked(i, carry):
        rows = pl.ds(pl.multiple_of(i * 128, 128), 128)
        half_table[rows, :] = jnp.dot(
            picker[rows, :], table_in[...], preferred_element_type=jnp.float32
        ).astype(jnp.bfloat16)
        return carry

    lax.fori_loop(0, OWN, rows_picked, 0)

    def columns_picked(i, carry):
        rows = pl.ds(pl.multiple_of(i * 128, 128), 128)
        full = jnp.dot(half_table[rows, :], picker_t[...], preferred_element_type=jnp.float32)
        table[rows, :] = full.astype(jnp.bfloat16)
        for j in range(OWN):
            table_t[pl.ds(j * 128, 128), rows] = full[:, j * 128 : (j + 1) * 128].T.astype(jnp.bfloat16)
        return carry

    lax.fori_loop(0, OWN, columns_picked, 0)

    tile_sea = sea_mask[pl.ds(pl.multiple_of(z * 8, 8), 8), :].astype(jnp.float32)
    column = lax.broadcasted_iota(jnp.int32, (128, 128), 0)
    target = lax.broadcasted_iota(jnp.int32, (128, 128), 1)
    spread = jnp.where(column == q * TILE + target % TILE, 1.0, 0.0)
    tile_sea = jnp.dot(tile_sea, spread, preferred_element_type=jnp.float32)
    inner = lax.broadcasted_iota(jnp.int32, (8, 128), 0)
    tile_sea = jnp.sum(jnp.where(inner == block, tile_sea, 0.0), axis=0, keepdims=True)

    pltpu.make_async_copy(spectrum, spectrum, recv_sem).wait()
    for j in range(OWN):
        rows = pl.ds(j * WIDE, WIDE)
        value = inbox[pl.ds(j, WIDE, stride=PAD), :]
        moved[rows, :] = value
        rounded[rows, :] = value.astype(jnp.bfloat16)
        square[rows, :] = (value * value).astype(jnp.bfloat16)

    def interact(rows):
        value = moved[rows, :]
        gain = value * jnp.dot(table[rows, :], rounded[...], preferred_element_type=jnp.float32)
        loss = jnp.dot(table_t[rows, :], square[...], preferred_element_type=jnp.float32)
        return tile_sea * jnp.maximum(value + time_step * (gain - loss), 0.0)

    lane_g = lax.broadcasted_iota(jnp.int32, (GROUP, 128), 1)
    lane_h = lax.broadcasted_iota(jnp.int32, (HALF, 128), 1)
    for g in range(8):
        rows = pl.ds(g * GROUP, GROUP)
        value = interact(rows)
        energy[rows, :] = value
        north = pltpu.roll(value, (TILE * (g + 1)) % 128, 1) if g < 7 else value
        south = pltpu.roll(value, TILE * g, 1) if g else value
        here = lane_g // TILE == g
        if g:
            north = jnp.where(here, north, row_out[0])
            south = jnp.where(here, south, row_out[1])
        row_out[0] = north
        row_out[1] = south
        for u in range(2):
            b = 2 * g + u
            part = value[u * HALF : (u + 1) * HALF]
            east = pltpu.roll(part, (b + 113) % 128, 1) if b != 15 else part
            west = pltpu.roll(part, b, 1) if b else part
            here = lane_h % TILE == b
            if b:
                east = jnp.where(here, east, col_out[0])
                west = jnp.where(here, west, col_out[1])
            col_out[0] = east
            col_out[1] = west

    edges = []
    for e, (source, sink, side, there) in enumerate(
        (
            (row_out, row_in, 0, north_id),
            (row_out, row_in, 1, south_id),
            (col_out, col_in, 0, east_id),
            (col_out, col_in, 1, west_id),
        )
    ):
        edges.append(
            pltpu.make_async_remote_copy(
                src_ref=source.at[side],
                dst_ref=sink.at[side],
                send_sem=edge_send.at[e],
                recv_sem=edge_recv.at[e],
                device_id=there,
                device_id_type=MESH,
            )
        )
        edges[-1].start()
    for edge in edges:
        edge.wait()

    has_south = jnp.logical_or(slab > 0, z > 0)
    has_north = jnp.logical_or(slab < 3, z < 15)
    keep_south = jnp.where(has_south, 1.0, 0.0)
    keep_north = jnp.where(has_north, 1.0, 0.0)
    for b in range(16):
        g, u = b // 2, b % 2
        rows = pl.ds(b * HALF, HALF)
        packed = pl.ds(u * HALF, HALF)
        value = energy[rows, :]
        west = col_in[0]
        west = pltpu.roll(west, 128 - b, 1) if b else west
        west = jnp.where(lane_h % TILE == 0, west, pltpu.roll(value, 1, 1))
        east = col_in[1]
        east = pltpu.roll(east, 15 - b, 1) if b != 15 else east
        east = jnp.where(lane_h % TILE == TILE - 1, east, pltpu.roll(value, 127, 1))
        south = keep_south * row_in[0, packed, :]
        south = pltpu.roll(south, 128 - TILE * g, 1) if g else south
        south = jnp.where(lane_h < TILE, south, pltpu.roll(value, TILE, 1))
        north = keep_north * row_in[1, packed, :]
        north = pltpu.roll(north, 112 - TILE * g, 1) if g < 7 else north
        north = jnp.where(lane_h >= 112, north, pltpu.roll(value, 112, 1))
        e, n = east_wide[rows, :], north_wide[rows, :]
        result = (1.0 - jnp.abs(e) - jnp.abs(n)) * value + jnp.maximum(e, 0.0) * west
        result = result + jnp.maximum(-e, 0.0) * east
        result = result + jnp.maximum(n, 0.0) * south
        result = result + jnp.maximum(-n, 0.0) * north
        moved[rows, :] = result
    for j in range(OWN):
        rows = pl.ds(j * WIDE, WIDE)
        value = moved[rows, :]
        rounded[rows, :] = value.astype(jnp.bfloat16)
        square[rows, :] = (value * value).astype(jnp.bfloat16)
    for j in range(OWN):
        outbox2[pl.ds(j, WIDE, stride=PAD), :] = interact(pl.ds(j * WIDE, WIDE))

    def send_back(step, carry):
        peer = peer_of(me, step)
        pltpu.make_async_remote_copy(
            src_ref=outbox2.at[pl.ds(pl.multiple_of(peer * PAD, PAD), OWN)],
            dst_ref=inbox2.at[my_tile],
            send_sem=send_sem2,
            recv_sem=recv_sem2,
            device_id={"slab": slab, "wide": peer},
            device_id_type=MESH,
        ).start()
        return carry

    lax.fori_loop(1, WIDE, send_back, 0)
    pltpu.make_async_copy(outbox2.at[mine], inbox2.at[my_tile], recv_sem2).start()
    pltpu.make_async_copy(spectrum, spectrum, recv_sem2).wait()

    def unpack(j, carry):
        for h in range(2):
            parts = [inbox2[pl.ds(h * 128 + k * PAD + j, 8, stride=256), :] for k in range(8)]
            for k, part in enumerate(swap_blocks(parts, block)):
                out[j, pl.ds(8 * h + k, 8, stride=16), :] = part
        return carry

    lax.fori_loop(0, OWN, unpack, 0)
    for sem in (send_sem, send_sem2):
        most = plane.at[pl.ds(0, OWN - 1), pl.ds(0, ROWS)]
        pltpu.make_async_copy(most, most, sem).wait()
        rest = plane.at[0, pl.ds(0, ROWS - OWN)]
        pltpu.make_async_copy(rest, rest, sem).wait()


def velocities(slot_owner, courant):
    band_count = courant.shape[0]
    heading = slot_owner % ND
    freq_band = slot_owner // ND
    picked = freq_band[..., None] == jnp.arange(band_count, dtype=jnp.int32)
    wave_speed = jnp.sum(jnp.where(picked, courant, 0.0), axis=-1)
    wave_angle = heading.astype(jnp.float32) * (2.0 * math.pi / ND)
    return wave_speed * jnp.cos(wave_angle), wave_speed * jnp.sin(wave_angle)


def body(spectrum, sea_mask, courant, slot_owner, coupling):
    me = lax.axis_index("wide")
    east, north = velocities(lax.dynamic_slice_in_dim(slot_owner, me * OWN, OWN), courant)
    own_speed = jnp.concatenate(
        [
            1.0 - jnp.abs(east) - jnp.abs(north),
            jnp.maximum(east, 0.0),
            jnp.maximum(-east, 0.0),
            jnp.maximum(north, 0.0),
            jnp.maximum(-north, 0.0),
        ]
    )
    owner = slot_owner.reshape(WIDE, OWN).T
    slot_speed = jnp.concatenate(velocities(owner, courant))
    vmem = pl.BlockSpec(memory_space=pltpu.VMEM)
    anywhere = pl.BlockSpec(memory_space=pl.ANY)
    f32, bf16, dma = jnp.float32, jnp.bfloat16, pltpu.SemaphoreType.DMA
    mailbox = pltpu.VMEM((WIDE * PAD, 128), f32)
    square_table = pltpu.VMEM((SLOTS, SLOTS), bf16)
    column = pltpu.VMEM((SLOTS, 128), f32)
    return pl.pallas_call(
        kernel,
        out_shape=jax.ShapeDtypeStruct((OWN, ROWS, 128), f32),
        in_specs=[anywhere, vmem, pl.BlockSpec(memory_space=pltpu.SMEM), vmem, vmem, anywhere],
        out_specs=vmem,
        scratch_shapes=[
            pltpu.VMEM((OWN, HOLD, 128), f32),
            square_table,
            mailbox,
            mailbox,
            mailbox,
            mailbox,
            pltpu.VMEM((2, 16, 128), f32),
            pltpu.VMEM((2, 16, 128), f32),
            square_table,
            square_table,
            square_table,
            square_table,
            square_table,
            column,
            column,
            column,
            column,
            pltpu.VMEM((SLOTS, 128), bf16),
            pltpu.VMEM((SLOTS, 128), bf16),
            column,
            pltpu.VMEM((2, GROUP, 128), f32),
            pltpu.VMEM((2, GROUP, 128), f32),
            pltpu.VMEM((2, HALF, 128), f32),
            pltpu.VMEM((2, HALF, 128), f32),
            dma,
            dma,
            dma,
            dma,
            dma,
            dma,
            dma((2,)),
            dma((2,)),
            dma((4,)),
            dma((4,)),
        ],
        compiler_params=pltpu.CompilerParams(
            collective_id=0, has_side_effects=True, vmem_limit_bytes=48 << 20
        ),
    )(spectrum, sea_mask, own_speed, slot_speed, owner.astype(f32), coupling)


def solution(mesh):
    return jax.shard_map(
        body,
        mesh=mesh,
        in_specs=(P("wide", "slab", None), P("slab", None), P(), P(), P()),
        out_specs=P("wide", "slab", None),
        check_vma=False,
    )
```

```python
import math

import jax
import jax.numpy as jnp
from jax import lax
from jax.experimental import pallas as pl
from jax.experimental.pallas import tpu as pltpu
from jax.sharding import PartitionSpec as P

ND = 36
NF = 32
WIDE = 128
OWN = 9
PAD = 16
SLOTS = OWN * WIDE
ROWS = 128
HOLD = 144
TOP = 8
TILE = 16
GROUP = 144
HALF = 72
EARLY = 32
FIRST = 2
MESH = pl.DeviceIdType.MESH

time_step = 0.5


def place(me):
    return me // 64, (me // 4) % 16, me % 4


def tile_of(y, x):
    return jnp.where(y == 0, x, 7 - x)


def device_of(z, q):
    y = q // 4
    return y * 64 + z * 4 + jnp.where(y == 0, q, 7 - q)


def peer_of(me, step):
    y, z, x = place(me)
    turn, plane = step % 16, step // 16
    half = (turn + 1) // 2
    dz = jnp.where(turn % 2 == 1, half, 16 - half)
    return ((y + plane // 4) % 2) * 64 + ((z + dz) % 16) * 4 + (x + plane % 4) % 4


def swap_blocks(parts, block):
    parts = list(parts)
    for bit in (4, 2, 1):
        high = (block & bit) != 0
        for a in range(8):
            if a & bit:
                continue
            first, second = parts[a], parts[a + bit]
            parts[a] = jnp.where(high, pltpu.roll(second, TILE * bit, 1), first)
            parts[a + bit] = jnp.where(high, second, pltpu.roll(first, 128 - TILE * bit, 1))
    return parts


def kernel(
    spectrum,
    sea_hbm,
    courant_hbm,
    owner_hbm,
    coupling,
    out,
    sea_mask,
    courant,
    owner_scalar,
    owner_rows,
    owner,
    own_speed,
    natural,
    plane,
    table_in,
    outbox,
    inbox,
    outbox2,
    inbox2,
    rim_out,
    rim_in,
    picker,
    picker_t,
    half_table,
    table,
    table_t,
    owner_wide,
    east_wide,
    north_wide,
    moved,
    rounded,
    square,
    energy,
    row_out,
    row_in,
    col_out,
    col_in,
    load_sem,
    sea_sem,
    small_sem,
    table_sem,
    send_sem,
    recv_sem,
    send_sem2,
    recv_sem2,
    rim_send,
    rim_recv,
    edge_send,
    edge_recv,
):
    slab = lax.axis_index("slab")
    me = lax.axis_index("wide")
    y, z, x = place(me)
    q = tile_of(y, x)
    spot = z * 8 + q
    up_slab, down_slab = (slab + 1) % 4, (slab + 3) % 4
    north_id = {
        "slab": jnp.where(z == 15, up_slab, slab),
        "wide": y * 64 + ((z + 1) % 16) * 4 + x,
    }
    south_id = {
        "slab": jnp.where(z == 0, down_slab, slab),
        "wide": y * 64 + ((z + 15) % 16) * 4 + x,
    }
    east_id = {"slab": slab, "wide": device_of(z, (q + 1) % 8)}
    west_id = {"slab": slab, "wide": device_of(z, (q + 7) % 8)}

    small_loads = [
        pltpu.make_async_copy(owner_hbm, owner_scalar, small_sem.at[0]),
        pltpu.make_async_copy(courant_hbm, courant, small_sem.at[1]),
        pltpu.make_async_copy(owner_hbm, owner_rows, small_sem.at[2]),
    ]
    sea_load = pltpu.make_async_copy(sea_hbm, sea_mask, sea_sem)
    for load in (*small_loads, sea_load):
        load.start()
    loads = pltpu.make_async_copy(spectrum, plane.at[:, pl.ds(TOP, ROWS)], load_sem)
    loads.start()
    table_load = pltpu.make_async_copy(coupling, table_in, table_sem)
    table_load.start()

    barrier = pltpu.get_barrier_semaphore()
    for there in (
        {"slab": up_slab, "wide": me},
        {"slab": down_slab, "wide": me},
        north_id,
        south_id,
    ):
        pl.semaphore_signal(barrier, inc=1, device_id=there, device_id_type=MESH)

    def greet(step):
        pl.semaphore_signal(
            barrier, inc=1, device_id={"slab": slab, "wide": peer_of(me, step)}, device_id_type=MESH
        )

    greet(WIDE - 1)
    for load in small_loads:
        load.wait()
    row16 = lax.broadcasted_iota(jnp.int32, (16, 128), 0)
    own_angle = jnp.zeros((16, 128), jnp.float32)
    own_courant = jnp.zeros((16, 128), jnp.float32)
    for j in range(OWN):
        slot = me * OWN + j
        component = owner_scalar[slot // 128, slot % 128]
        freq = component // ND
        angle = (component - freq * ND).astype(jnp.float32) * (2.0 * math.pi / ND)
        own_angle = jnp.where(row16 == j, angle, own_angle)
        own_courant = jnp.where(row16 == j, courant[0, freq], own_courant)
    east, north = own_courant * jnp.cos(own_angle), own_courant * jnp.sin(own_angle)
    own_speed[0] = 1.0 - jnp.abs(east) - jnp.abs(north)
    own_speed[1] = jnp.maximum(east, 0.0)
    own_speed[2] = jnp.maximum(-east, 0.0)
    own_speed[3] = jnp.maximum(north, 0.0)
    own_speed[4] = jnp.maximum(-north, 0.0)

    lane = lax.broadcasted_iota(jnp.int32, (8, 128), 1)
    block = lane // TILE

    sea_load.wait()
    loads.wait()
    sea = sea_mask[...].astype(jnp.float32)
    for j in range(OWN):
        plane[j, pl.ds(TOP, ROWS), :] = plane[j, pl.ds(TOP, ROWS), :] * sea
        plane[j, pl.ds(TOP - 8, 8), :] = jnp.zeros((8, 128), jnp.float32)
        plane[j, pl.ds(TOP + ROWS, 8), :] = jnp.zeros((8, 128), jnp.float32)
        rim_out[0, pl.ds(j, 1), :] = own_speed[3, pl.ds(j, 1), :] * plane[j, pl.ds(TOP + ROWS - 1, 1), :]
        rim_out[1, pl.ds(j, 1), :] = own_speed[4, pl.ds(j, 1), :] * plane[j, pl.ds(TOP, 1), :]

    def propagate(j, carry):
        for u in range(14):
            greet(j * 14 + u + 1)
        remain, east, west, north, south = [own_speed[u, pl.ds(j, 1), :] for u in range(5)]
        for h in range(2):
            parts = []
            for k in range(8):
                start = TOP + 8 * h + k
                here = plane[j, pl.ds(start, 8, stride=16), :]
                part = remain * here + east * pltpu.roll(here, 1, 1)
                part = part + west * pltpu.roll(here, 127, 1)
                part = part + north * plane[j, pl.ds(start - 1, 8, stride=16), :]
                parts.append(part + south * plane[j, pl.ds(start + 1, 8, stride=16), :])
            for k, part in enumerate(swap_blocks(parts, block)):
                outbox[pl.ds(h * 128 + k * PAD + j, 8, stride=256), :] = part
        return carry

    lax.fori_loop(0, OWN, propagate, 0)

    pl.semaphore_wait(barrier, WIDE - 1 + 4)

    rims = []
    for side, there in ((0, up_slab), (1, down_slab)):
        rims.append(
            pltpu.make_async_remote_copy(
                src_ref=rim_out.at[side, pl.ds(0, OWN)],
                dst_ref=rim_in.at[side, pl.ds(0, OWN)],
                send_sem=rim_send.at[side],
                recv_sem=rim_recv.at[side],
                device_id={"slab": there, "wide": me},
                device_id_type=MESH,
            )
        )
        rims[-1].start()
    mine = pl.ds(pl.multiple_of(me * PAD, PAD), OWN)
    my_tile = pl.ds(pl.multiple_of(spot * PAD, PAD), OWN)

    def send(step, carry):
        peer = peer_of(me, step)
        py, pz, px = place(peer)
        row = (pz * 8 + tile_of(py, px)) * PAD
        pltpu.make_async_remote_copy(
            src_ref=outbox.at[pl.ds(pl.multiple_of(row, PAD), OWN)],
            dst_ref=inbox.at[mine],
            send_sem=send_sem,
            recv_sem=recv_sem,
            device_id={"slab": slab, "wide": peer},
            device_id_type=MESH,
        ).start()
        return carry

    def send_inner(step, carry):
        _, pz, _ = place(peer_of(me, step))

        @pl.when(jnp.logical_and(pz > 0, pz < 15))
        def _():
            send(step, 0)

        return carry

    def send_outer(step, carry):
        _, pz, _ = place(peer_of(me, step))

        @pl.when(jnp.logical_or(pz == 0, pz == 15))
        def _():
            send(step, 0)

        return carry

    lax.fori_loop(1, EARLY, send_inner, 0)
    for rim in rims:
        rim.wait()
    lane9 = lax.broadcasted_iota(jnp.int32, (OWN, 128), 1)
    below = jnp.where(slab > 0, 1.0, 0.0) * rim_in[0, pl.ds(0, OWN), :]
    above = jnp.where(slab < 3, 1.0, 0.0) * rim_in[1, pl.ds(0, OWN), :]
    for k in range(8):
        low = pltpu.roll(below, (128 - TILE * k) % 128, 1) if k else below
        rows = pl.ds(k * PAD, OWN)
        outbox[rows, :] = outbox[rows, :] + jnp.where(lane9 < TILE, low, 0.0)
        high = pltpu.roll(above, 112 - TILE * k, 1) if k < 7 else above
        rows = pl.ds((15 * 8 + k) * PAD, OWN)
        outbox[rows, :] = outbox[rows, :] + jnp.where(lane9 >= 112, high, 0.0)
    lax.fori_loop(1, EARLY, send_outer, 0)
    lax.fori_loop(EARLY, WIDE, send, 0)
    pltpu.make_async_copy(outbox.at[my_tile], inbox.at[mine], recv_sem).start()

    owners = owner_rows[...].astype(jnp.float32)
    band = jnp.floor((owners + 0.5) * (1.0 / ND))
    angle = (owners - band * ND) * (2.0 * math.pi / ND)
    speed = jnp.zeros((OWN, 128), jnp.float32)
    for f in range(NF):
        speed = jnp.where(band == f, courant[0, f], speed)
    wide_rows = (owners, speed * jnp.cos(angle), speed * jnp.sin(angle))
    for wide_form, row_form in zip((owner_wide, east_wide, north_wide), wide_rows):
        for j in range(OWN):
            natural[pl.ds(j * 128, 128), :] = jnp.broadcast_to(row_form[j : j + 1], (128, 128)).T
        for j in range(OWN):
            wide_form[pl.ds(j * WIDE, WIDE), :] = natural[pl.ds(j, WIDE, stride=OWN), :]
    for j in range(OWN):
        owner[pl.ds(j, 1), :] = owner_wide[pl.ds(j * WIDE, WIDE), :].T[0:1]

    lanes = lax.broadcasted_iota(jnp.int32, (128, 128), 1).astype(jnp.float32)
    sublanes = lax.broadcasted_iota(jnp.int32, (128, 128), 0).astype(jnp.float32)

    def pick(i, carry):
        rows = pl.ds(pl.multiple_of(i * 128, 128), 128)
        base = (i * 128).astype(jnp.float32)
        for j in range(OWN):
            columns = pl.ds(j * 128, 128)
            hit = owner_wide[rows, :] == lanes + 128.0 * j
            picker[rows, columns] = jnp.where(hit, 1.0, 0.0).astype(jnp.bfloat16)
            hit = owner[pl.ds(j, 1), :] == sublanes + base
            picker_t[rows, columns] = jnp.where(hit, 1.0, 0.0).astype(jnp.bfloat16)
        return carry

    lax.fori_loop(0, OWN, pick, 0)
    table_load.wait()

    def rows_picked(i, carry):
        rows = pl.ds(pl.multiple_of(i * 128, 128), 128)
        half_table[rows, :] = jnp.dot(
            picker[rows, :], table_in[...], preferred_element_type=jnp.float32
        ).astype(jnp.bfloat16)
        return carry

    lax.fori_loop(0, OWN, rows_picked, 0)

    def columns_picked(i, carry):
        rows = pl.ds(pl.multiple_of(i * 128, 128), 128)
        full = jnp.dot(half_table[rows, :], picker_t[...], preferred_element_type=jnp.float32)
        table[rows, :] = full.astype(jnp.bfloat16)
        for j in range(OWN):
            table_t[pl.ds(j * 128, 128), rows] = full[:, j * 128 : (j + 1) * 128].T.astype(jnp.bfloat16)
        return carry

    lax.fori_loop(0, OWN, columns_picked, 0)

    tile_sea = sea_mask[pl.ds(pl.multiple_of(z * 8, 8), 8), :].astype(jnp.float32)
    column = lax.broadcasted_iota(jnp.int32, (128, 128), 0)
    target = lax.broadcasted_iota(jnp.int32, (128, 128), 1)
    spread = jnp.where(column == q * TILE + target % TILE, 1.0, 0.0)
    tile_sea = jnp.dot(tile_sea, spread, preferred_element_type=jnp.float32)
    inner = lax.broadcasted_iota(jnp.int32, (8, 128), 0)
    tile_sea = jnp.sum(jnp.where(inner == block, tile_sea, 0.0), axis=0, keepdims=True)

    pltpu.make_async_copy(spectrum, spectrum, recv_sem).wait()
    for j in range(OWN):
        rows = pl.ds(j * WIDE, WIDE)
        value = inbox[pl.ds(j, WIDE, stride=PAD), :]
        moved[rows, :] = value
        rounded[rows, :] = value.astype(jnp.bfloat16)
        square[rows, :] = (value * value).astype(jnp.bfloat16)

    def interact(rows):
        value = moved[rows, :]
        gain = value * jnp.dot(table[rows, :], rounded[...], preferred_element_type=jnp.float32)
        loss = jnp.dot(table_t[rows, :], square[...], preferred_element_type=jnp.float32)
        return tile_sea * jnp.maximum(value + time_step * (gain - loss), 0.0)

    lane_g = lax.broadcasted_iota(jnp.int32, (GROUP, 128), 1)
    lane_h = lax.broadcasted_iota(jnp.int32, (HALF, 128), 1)
    for g in range(8):
        rows = pl.ds(g * GROUP, GROUP)
        value = interact(rows)
        energy[rows, :] = value
        north = pltpu.roll(value, (TILE * (g + 1)) % 128, 1) if g < 7 else value
        south = pltpu.roll(value, TILE * g, 1) if g else value
        here = lane_g // TILE == g
        if g:
            north = jnp.where(here, north, row_out[0])
            south = jnp.where(here, south, row_out[1])
        row_out[0] = north
        row_out[1] = south
        for u in range(2):
            b = 2 * g + u
            part = value[u * HALF : (u + 1) * HALF]
            east = pltpu.roll(part, (b + 113) % 128, 1) if b != 15 else part
            west = pltpu.roll(part, b, 1) if b else part
            here = lane_h % TILE == b
            if b:
                east = jnp.where(here, east, col_out[0])
                west = jnp.where(here, west, col_out[1])
            col_out[0] = east
            col_out[1] = west

    edges = []
    for e, (source, sink, side, there) in enumerate(
        (
            (row_out, row_in, 0, north_id),
            (row_out, row_in, 1, south_id),
            (col_out, col_in, 0, east_id),
            (col_out, col_in, 1, west_id),
        )
    ):
        edges.append(
            pltpu.make_async_remote_copy(
                src_ref=source.at[side],
                dst_ref=sink.at[side],
                send_sem=edge_send.at[e],
                recv_sem=edge_recv.at[e],
                device_id=there,
                device_id_type=MESH,
            )
        )
        edges[-1].start()
    for edge in edges:
        edge.wait()

    has_south = jnp.logical_or(slab > 0, z > 0)
    has_north = jnp.logical_or(slab < 3, z < 15)
    keep_south = jnp.where(has_south, 1.0, 0.0)
    keep_north = jnp.where(has_north, 1.0, 0.0)
    for b in range(16):
        g, u = b // 2, b % 2
        rows = pl.ds(b * HALF, HALF)
        packed = pl.ds(u * HALF, HALF)
        value = energy[rows, :]
        west = col_in[0]
        west = pltpu.roll(west, 128 - b, 1) if b else west
        west = jnp.where(lane_h % TILE == 0, west, pltpu.roll(value, 1, 1))
        east = col_in[1]
        east = pltpu.roll(east, 15 - b, 1) if b != 15 else east
        east = jnp.where(lane_h % TILE == TILE - 1, east, pltpu.roll(value, 127, 1))
        south = keep_south * row_in[0, packed, :]
        south = pltpu.roll(south, 128 - TILE * g, 1) if g else south
        south = jnp.where(lane_h < TILE, south, pltpu.roll(value, TILE, 1))
        north = keep_north * row_in[1, packed, :]
        north = pltpu.roll(north, 112 - TILE * g, 1) if g < 7 else north
        north = jnp.where(lane_h >= 112, north, pltpu.roll(value, 112, 1))
        e, n = east_wide[rows, :], north_wide[rows, :]
        result = (1.0 - jnp.abs(e) - jnp.abs(n)) * value + jnp.maximum(e, 0.0) * west
        result = result + jnp.maximum(-e, 0.0) * east
        result = result + jnp.maximum(n, 0.0) * south
        result = result + jnp.maximum(-n, 0.0) * north
        moved[rows, :] = result
    for j in range(OWN):
        rows = pl.ds(j * WIDE, WIDE)
        value = moved[rows, :]
        rounded[rows, :] = value.astype(jnp.bfloat16)
        square[rows, :] = (value * value).astype(jnp.bfloat16)
    for j in range(OWN):
        outbox2[pl.ds(j, WIDE, stride=PAD), :] = interact(pl.ds(j * WIDE, WIDE))

    def send_back(step, carry):
        peer = peer_of(me, step)
        pltpu.make_async_remote_copy(
            src_ref=outbox2.at[pl.ds(pl.multiple_of(peer * PAD, PAD), OWN)],
            dst_ref=inbox2.at[my_tile],
            send_sem=send_sem2,
            recv_sem=recv_sem2,
            device_id={"slab": slab, "wide": peer},
            device_id_type=MESH,
        ).start()
        return carry

    def send_first(step, carry):
        _, pz, _ = place(peer_of(me, step))

        @pl.when(pz < FIRST)
        def _():
            send_back(step, 0)

        return carry

    def send_later(step, carry):
        _, pz, _ = place(peer_of(me, step))

        @pl.when(pz >= FIRST)
        def _():
            send_back(step, 0)

        return carry

    lax.fori_loop(1, WIDE, send_first, 0)
    lax.fori_loop(1, WIDE, send_later, 0)
    pltpu.make_async_copy(outbox2.at[mine], inbox2.at[my_tile], recv_sem2).start()
    pltpu.make_async_copy(spectrum, spectrum, recv_sem2).wait()

    def unpack(j, carry):
        for h in range(2):
            parts = [inbox2[pl.ds(h * 128 + k * PAD + j, 8, stride=256), :] for k in range(8)]
            for k, part in enumerate(swap_blocks(parts, block)):
                out[j, pl.ds(8 * h + k, 8, stride=16), :] = part
        return carry

    lax.fori_loop(0, OWN, unpack, 0)
    for sem in (send_sem, send_sem2):
        most = plane.at[pl.ds(0, OWN - 1), pl.ds(0, ROWS)]
        pltpu.make_async_copy(most, most, sem).wait()
        rest = plane.at[0, pl.ds(0, ROWS - OWN)]
        pltpu.make_async_copy(rest, rest, sem).wait()


def body(spectrum, sea_mask, courant, slot_owner, coupling):
    vmem = pl.BlockSpec(memory_space=pltpu.VMEM)
    anywhere = pl.BlockSpec(memory_space=pltpu.HBM)
    f32, bf16, dma = jnp.float32, jnp.bfloat16, pltpu.SemaphoreType.DMA
    mailbox = pltpu.VMEM((WIDE * PAD, 128), f32)
    square_table = pltpu.VMEM((SLOTS, SLOTS), bf16)
    column = pltpu.VMEM((SLOTS, 128), f32)
    return pl.pallas_call(
        kernel,
        out_shape=jax.ShapeDtypeStruct((OWN, ROWS, 128), f32),
        in_specs=[anywhere] * 5,
        out_specs=vmem,
        scratch_shapes=[
            pltpu.VMEM((ROWS, 128), jnp.int32),
            pltpu.SMEM((1, NF), f32),
            pltpu.SMEM((OWN, 128), jnp.int32),
            pltpu.VMEM((OWN, 128), jnp.int32),
            pltpu.VMEM((16, 128), f32),
            pltpu.VMEM((5, 16, 128), f32),
            column,
            pltpu.VMEM((OWN, HOLD, 128), f32),
            square_table,
            mailbox,
            mailbox,
            mailbox,
            mailbox,
            pltpu.VMEM((2, 16, 128), f32),
            pltpu.VMEM((2, 16, 128), f32),
            square_table,
            square_table,
            square_table,
            square_table,
            square_table,
            column,
            column,
            column,
            column,
            pltpu.VMEM((SLOTS, 128), bf16),
            pltpu.VMEM((SLOTS, 128), bf16),
            column,
            pltpu.VMEM((2, GROUP, 128), f32),
            pltpu.VMEM((2, GROUP, 128), f32),
            pltpu.VMEM((2, HALF, 128), f32),
            pltpu.VMEM((2, HALF, 128), f32),
            dma,
            dma,
            dma((3,)),
            dma,
            dma,
            dma,
            dma,
            dma,
            dma((2,)),
            dma((2,)),
            dma((4,)),
            dma((4,)),
        ],
        compiler_params=pltpu.CompilerParams(
            collective_id=0, has_side_effects=True, vmem_limit_bytes=60 << 20
        ),
    )(spectrum, sea_mask, courant.reshape(1, NF), slot_owner.reshape(OWN, 128), coupling)


def solution(mesh):
    return jax.shard_map(
        body,
        mesh=mesh,
        in_specs=(P("wide", "slab", None), P("slab", None), P(), P(), P()),
        out_specs=P("wide", "slab", None),
        check_vma=False,
    )
```

```python
import math

import jax
import jax.numpy as jnp
from jax import lax
from jax.experimental import pallas as pl
from jax.experimental.pallas import tpu as pltpu
from jax.sharding import PartitionSpec as P

ND = 36
NF = 32
WIDE = 128
OWN = 9
PAD = 16
SLOTS = OWN * WIDE
ROWS = 128
HOLD = 144
TOP = 8
TILE = 16
GROUP = 144
HALF = 72
EARLY = 5
FIRST = 4
MESH = pl.DeviceIdType.MESH

time_step = 0.5


def place(me):
    return me // 64, (me // 4) % 16, me % 4


def tile_of(y, x):
    return jnp.where(y == 0, x, 7 - x)


def device_of(z, q):
    y = q // 4
    return y * 64 + z * 4 + jnp.where(y == 0, q, 7 - q)


def distance(turn):
    far = 8 - (turn + 1) // 2
    return lax.rem(jnp.where(lax.rem(turn, 2) == 1, far, 16 - far), 16)


def swap_blocks(parts, block):
    parts = list(parts)
    for bit in (4, 2, 1):
        high = (block & bit) != 0
        for a in range(8):
            if a & bit:
                continue
            first, second = parts[a], parts[a + bit]
            parts[a] = jnp.where(high, pltpu.roll(second, TILE * bit, 1), first)
            parts[a + bit] = jnp.where(high, second, pltpu.roll(first, 128 - TILE * bit, 1))
    return parts


def kernel(
    spectrum,
    sea_hbm,
    courant_hbm,
    owner_hbm,
    coupling,
    inbox2,
    sea_mask,
    courant,
    owner_scalar,
    owner_rows,
    owner,
    own_speed,
    natural,
    plane,
    table_in,
    outbox,
    inbox,
    outbox2,
    rim_out,
    rim_in,
    picker,
    picker_t,
    half_table,
    table,
    table_t,
    owner_wide,
    east_wide,
    north_wide,
    moved,
    rounded,
    square,
    energy,
    row_out,
    row_in,
    col_out,
    col_in,
    load_sem,
    sea_sem,
    small_sem,
    table_sem,
    send_sem,
    recv_sem,
    send_sem2,
    recv_sem2,
    rim_send,
    rim_recv,
    edge_send,
    edge_recv,
):
    slab = lax.axis_index("slab")
    me = lax.axis_index("wide")
    y, z, x = place(me)
    q = tile_of(y, x)
    spot = z * 8 + q
    places = []
    for p in range(8):
        py, px = lax.rem(y + p // 4, 2), lax.rem(x + p % 4, 4)
        places.append((py * 64 + px, tile_of(py, px)))
    up_slab, down_slab = (slab + 1) % 4, (slab + 3) % 4
    north_id = {
        "slab": jnp.where(z == 15, up_slab, slab),
        "wide": y * 64 + ((z + 1) % 16) * 4 + x,
    }
    south_id = {
        "slab": jnp.where(z == 0, down_slab, slab),
        "wide": y * 64 + ((z + 15) % 16) * 4 + x,
    }
    east_id = {"slab": slab, "wide": device_of(z, (q + 1) % 8)}
    west_id = {"slab": slab, "wide": device_of(z, (q + 7) % 8)}

    small_loads = [
        pltpu.make_async_copy(owner_hbm, owner_scalar, small_sem.at[0]),
        pltpu.make_async_copy(courant_hbm, courant, small_sem.at[1]),
        pltpu.make_async_copy(owner_hbm, owner_rows, small_sem.at[2]),
    ]
    sea_load = pltpu.make_async_copy(sea_hbm, sea_mask, sea_sem)
    for load in (*small_loads, sea_load):
        load.start()
    loads = pltpu.make_async_copy(spectrum, plane.at[:, pl.ds(TOP, ROWS)], load_sem)
    loads.start()
    table_load = pltpu.make_async_copy(coupling, table_in, table_sem)
    table_load.start()

    barrier = pltpu.get_barrier_semaphore()
    for there in (
        {"slab": up_slab, "wide": me},
        {"slab": down_slab, "wide": me},
        north_id,
        south_id,
    ):
        pl.semaphore_signal(barrier, inc=1, device_id=there, device_id_type=MESH)

    def greet(turn, first=0):
        pz = lax.rem(z + distance(turn), 16) if first == 0 else z
        for base, _ in places[first:]:
            pl.semaphore_signal(
                barrier, inc=1, device_id={"slab": slab, "wide": base + pz * 4}, device_id_type=MESH
            )

    for turn in (0, 1, 2, 3, 13, 14):
        greet(turn)
    greet(0, 1)
    for load in small_loads:
        load.wait()
    row16 = lax.broadcasted_iota(jnp.int32, (16, 128), 0)
    own_angle = jnp.zeros((16, 128), jnp.float32)
    own_courant = jnp.zeros((16, 128), jnp.float32)
    for j in range(OWN):
        slot = me * OWN + j
        component = owner_scalar[slot // 128, slot % 128]
        freq = component // ND
        angle = (component - freq * ND).astype(jnp.float32) * (2.0 * math.pi / ND)
        own_angle = jnp.where(row16 == j, angle, own_angle)
        own_courant = jnp.where(row16 == j, courant[0, freq], own_courant)
    east, north = own_courant * jnp.cos(own_angle), own_courant * jnp.sin(own_angle)
    own_speed[0] = 1.0 - jnp.abs(east) - jnp.abs(north)
    own_speed[1] = jnp.maximum(east, 0.0)
    own_speed[2] = jnp.maximum(-east, 0.0)
    own_speed[3] = jnp.maximum(north, 0.0)
    own_speed[4] = jnp.maximum(-north, 0.0)

    lane = lax.broadcasted_iota(jnp.int32, (8, 128), 1)
    block = lane // TILE

    sea_load.wait()
    loads.wait()
    sea = sea_mask[...].astype(jnp.float32)
    for j in range(OWN):
        plane[j, pl.ds(TOP, ROWS), :] = plane[j, pl.ds(TOP, ROWS), :] * sea
        plane[j, pl.ds(TOP - 8, 8), :] = jnp.zeros((8, 128), jnp.float32)
        plane[j, pl.ds(TOP + ROWS, 8), :] = jnp.zeros((8, 128), jnp.float32)
        rim_out[0, pl.ds(j, 1), :] = own_speed[3, pl.ds(j, 1), :] * plane[j, pl.ds(TOP + ROWS - 1, 1), :]
        rim_out[1, pl.ds(j, 1), :] = own_speed[4, pl.ds(j, 1), :] * plane[j, pl.ds(TOP, 1), :]

    def propagate(j, carry):
        greet(j + 4)
        remain, east, west, north, south = [own_speed[u, pl.ds(j, 1), :] for u in range(5)]
        for h in range(2):
            parts = []
            for k in range(8):
                start = TOP + 8 * h + k
                here = plane[j, pl.ds(start, 8, stride=16), :]
                part = remain * here + east * pltpu.roll(here, 1, 1)
                part = part + west * pltpu.roll(here, 127, 1)
                part = part + north * plane[j, pl.ds(start - 1, 8, stride=16), :]
                parts.append(part + south * plane[j, pl.ds(start + 1, 8, stride=16), :])
            for k, part in enumerate(swap_blocks(parts, block)):
                outbox[pl.ds(h * 128 + k * PAD + j, 8, stride=256), :] = part
        return carry

    lax.fori_loop(0, OWN, propagate, 0)

    pl.semaphore_wait(barrier, WIDE - 1 + 4)

    rims = []
    for side, there in ((0, up_slab), (1, down_slab)):
        rims.append(
            pltpu.make_async_remote_copy(
                src_ref=rim_out.at[side, pl.ds(0, OWN)],
                dst_ref=rim_in.at[side, pl.ds(0, OWN)],
                send_sem=rim_send.at[side],
                recv_sem=rim_recv.at[side],
                device_id={"slab": there, "wide": me},
                device_id_type=MESH,
            )
        )
        rims[-1].start()
    mine = pl.ds(pl.multiple_of(me * PAD, PAD), OWN)
    my_tile = pl.ds(pl.multiple_of(spot * PAD, PAD), OWN)

    def send(pz, first=0):
        for base, tile in places[first:]:
            pltpu.make_async_remote_copy(
                src_ref=outbox.at[pl.ds(pl.multiple_of((pz * 8 + tile) * PAD, PAD), OWN)],
                dst_ref=inbox.at[mine],
                send_sem=send_sem,
                recv_sem=recv_sem,
                device_id={"slab": slab, "wide": base + pz * 4},
                device_id_type=MESH,
            ).start()

    def send_inner(turn, carry):
        pz = lax.rem(z + distance(turn), 16)

        @pl.when(jnp.logical_and(pz > 0, pz < 15))
        def _():
            send(pz)

        return carry

    def send_outer(turn, carry):
        pz = lax.rem(z + distance(turn), 16)

        @pl.when(jnp.logical_or(pz == 0, pz == 15))
        def _():
            send(pz)

        return carry

    def send_any(turn, carry):
        send(lax.rem(z + distance(turn), 16))
        return carry

    lax.fori_loop(0, EARLY, send_inner, 0)
    for rim in rims:
        rim.wait()
    lane9 = lax.broadcasted_iota(jnp.int32, (OWN, 128), 1)
    below = jnp.where(slab > 0, 1.0, 0.0) * rim_in[0, pl.ds(0, OWN), :]
    above = jnp.where(slab < 3, 1.0, 0.0) * rim_in[1, pl.ds(0, OWN), :]
    for k in range(8):
        low = pltpu.roll(below, (128 - TILE * k) % 128, 1) if k else below
        rows = pl.ds(k * PAD, OWN)
        outbox[rows, :] = outbox[rows, :] + jnp.where(lane9 < TILE, low, 0.0)
        high = pltpu.roll(above, 112 - TILE * k, 1) if k < 7 else above
        rows = pl.ds((15 * 8 + k) * PAD, OWN)
        outbox[rows, :] = outbox[rows, :] + jnp.where(lane9 >= 112, high, 0.0)
    lax.fori_loop(0, EARLY, send_outer, 0)
    lax.fori_loop(EARLY, 15, send_any, 0)
    send(z, 1)
    pltpu.make_async_copy(outbox.at[my_tile], inbox.at[mine], recv_sem).start()

    owners = owner_rows[...].astype(jnp.float32)
    band = jnp.floor((owners + 0.5) * (1.0 / ND))
    angle = (owners - band * ND) * (2.0 * math.pi / ND)
    speed = jnp.zeros((OWN, 128), jnp.float32)
    for f in range(NF):
        speed = jnp.where(band == f, courant[0, f], speed)
    wide_rows = (owners, speed * jnp.cos(angle), speed * jnp.sin(angle))
    for wide_form, row_form in zip((owner_wide, east_wide, north_wide), wide_rows):
        for j in range(OWN):
            natural[pl.ds(j * 128, 128), :] = jnp.broadcast_to(row_form[j : j + 1], (128, 128)).T
        for j in range(OWN):
            wide_form[pl.ds(j * WIDE, WIDE), :] = natural[pl.ds(j, WIDE, stride=OWN), :]
    for j in range(OWN):
        owner[pl.ds(j, 1), :] = owner_wide[pl.ds(j * WIDE, WIDE), :].T[0:1]

    lanes = lax.broadcasted_iota(jnp.int32, (128, 128), 1).astype(jnp.float32)
    sublanes = lax.broadcasted_iota(jnp.int32, (128, 128), 0).astype(jnp.float32)

    def pick(i, carry):
        rows = pl.ds(pl.multiple_of(i * 128, 128), 128)
        base = (i * 128).astype(jnp.float32)
        for j in range(OWN):
            columns = pl.ds(j * 128, 128)
            hit = owner_wide[rows, :] == lanes + 128.0 * j
            picker[rows, columns] = jnp.where(hit, 1.0, 0.0).astype(jnp.bfloat16)
            hit = owner[pl.ds(j, 1), :] == sublanes + base
            picker_t[rows, columns] = jnp.where(hit, 1.0, 0.0).astype(jnp.bfloat16)
        return carry

    lax.fori_loop(0, OWN, pick, 0)
    table_load.wait()

    def rows_picked(i, carry):
        rows = pl.ds(pl.multiple_of(i * 128, 128), 128)
        half_table[rows, :] = jnp.dot(
            picker[rows, :], table_in[...], preferred_element_type=jnp.float32
        ).astype(jnp.bfloat16)
        return carry

    lax.fori_loop(0, OWN, rows_picked, 0)

    def columns_picked(i, carry):
        rows = pl.ds(pl.multiple_of(i * 128, 128), 128)
        full = jnp.dot(half_table[rows, :], picker_t[...], preferred_element_type=jnp.float32)
        table[rows, :] = full.astype(jnp.bfloat16)
        for j in range(OWN):
            table_t[pl.ds(j * 128, 128), rows] = full[:, j * 128 : (j + 1) * 128].T.astype(jnp.bfloat16)
        return carry

    lax.fori_loop(0, OWN, columns_picked, 0)

    tile_sea = sea_mask[pl.ds(pl.multiple_of(z * 8, 8), 8), :].astype(jnp.float32)
    column = lax.broadcasted_iota(jnp.int32, (128, 128), 0)
    target = lax.broadcasted_iota(jnp.int32, (128, 128), 1)
    spread = jnp.where(column == q * TILE + target % TILE, 1.0, 0.0)
    tile_sea = jnp.dot(tile_sea, spread, preferred_element_type=jnp.float32)
    inner = lax.broadcasted_iota(jnp.int32, (8, 128), 0)
    tile_sea = jnp.sum(jnp.where(inner == block, tile_sea, 0.0), axis=0, keepdims=True)

    pltpu.make_async_copy(spectrum, spectrum, recv_sem).wait()
    for j in range(OWN):
        rows = pl.ds(j * WIDE, WIDE)
        value = inbox[pl.ds(j, WIDE, stride=PAD), :]
        moved[rows, :] = value
        rounded[rows, :] = value.astype(jnp.bfloat16)
        square[rows, :] = (value * value).astype(jnp.bfloat16)

    def interact(rows):
        value = moved[rows, :]
        gain = value * jnp.dot(table[rows, :], rounded[...], preferred_element_type=jnp.float32)
        loss = jnp.dot(table_t[rows, :], square[...], preferred_element_type=jnp.float32)
        return tile_sea * jnp.maximum(value + time_step * (gain - loss), 0.0)

    lane_g = lax.broadcasted_iota(jnp.int32, (GROUP, 128), 1)
    lane_h = lax.broadcasted_iota(jnp.int32, (HALF, 128), 1)
    for g in range(8):
        rows = pl.ds(g * GROUP, GROUP)
        value = interact(rows)
        energy[rows, :] = value
        north = pltpu.roll(value, (TILE * (g + 1)) % 128, 1) if g < 7 else value
        south = pltpu.roll(value, TILE * g, 1) if g else value
        here = lane_g // TILE == g
        if g:
            north = jnp.where(here, north, row_out[0])
            south = jnp.where(here, south, row_out[1])
        row_out[0] = north
        row_out[1] = south
        for u in range(2):
            b = 2 * g + u
            part = value[u * HALF : (u + 1) * HALF]
            east = pltpu.roll(part, (b + 113) % 128, 1) if b != 15 else part
            west = pltpu.roll(part, b, 1) if b else part
            here = lane_h % TILE == b
            if b:
                east = jnp.where(here, east, col_out[0])
                west = jnp.where(here, west, col_out[1])
            col_out[0] = east
            col_out[1] = west

    edges = []
    for e, (source, sink, side, there) in enumerate(
        (
            (row_out, row_in, 0, north_id),
            (row_out, row_in, 1, south_id),
            (col_out, col_in, 0, east_id),
            (col_out, col_in, 1, west_id),
        )
    ):
        edges.append(
            pltpu.make_async_remote_copy(
                src_ref=source.at[side],
                dst_ref=sink.at[side],
                send_sem=edge_send.at[e],
                recv_sem=edge_recv.at[e],
                device_id=there,
                device_id_type=MESH,
            )
        )
        edges[-1].start()
    for b in range(16):
        rows = pl.ds(b * HALF, HALF)
        value = energy[rows, :]
        west = jnp.where(lane_h % TILE == 0, 0.0, pltpu.roll(value, 1, 1))
        east = jnp.where(lane_h % TILE == TILE - 1, 0.0, pltpu.roll(value, 127, 1))
        south = jnp.where(lane_h < TILE, 0.0, pltpu.roll(value, TILE, 1))
        north = jnp.where(lane_h >= 112, 0.0, pltpu.roll(value, 112, 1))
        e, n = east_wide[rows, :], north_wide[rows, :]
        result = (1.0 - jnp.abs(e) - jnp.abs(n)) * value + jnp.maximum(e, 0.0) * west
        result = result + jnp.maximum(-e, 0.0) * east
        result = result + jnp.maximum(n, 0.0) * south
        moved[rows, :] = result + jnp.maximum(-n, 0.0) * north

    for edge in edges:
        edge.wait()

    has_south = jnp.logical_or(slab > 0, z > 0)
    has_north = jnp.logical_or(slab < 3, z < 15)
    keep_south = jnp.where(has_south, 1.0, 0.0)
    keep_north = jnp.where(has_north, 1.0, 0.0)
    for b in range(16):
        g, u = b // 2, b % 2
        rows = pl.ds(b * HALF, HALF)
        packed = pl.ds(u * HALF, HALF)
        west, east = col_in[0], col_in[1]
        west = pltpu.roll(west, 128 - b, 1) if b else west
        east = pltpu.roll(east, 15 - b, 1) if b != 15 else east
        south = keep_south * row_in[0, packed, :]
        south = pltpu.roll(south, 128 - TILE * g, 1) if g else south
        north = keep_north * row_in[1, packed, :]
        north = pltpu.roll(north, 112 - TILE * g, 1) if g < 7 else north
        e, n = east_wide[rows, :], north_wide[rows, :]
        result = moved[rows, :]
        result = result + jnp.where(lane_h % TILE == 0, jnp.maximum(e, 0.0) * west, 0.0)
        result = result + jnp.where(lane_h % TILE == TILE - 1, jnp.maximum(-e, 0.0) * east, 0.0)
        result = result + jnp.where(lane_h < TILE, jnp.maximum(n, 0.0) * south, 0.0)
        result = result + jnp.where(lane_h >= 112, jnp.maximum(-n, 0.0) * north, 0.0)
        moved[rows, :] = result
        if u:
            both = pl.ds(g * GROUP, GROUP)
            result = moved[both, :]
            rounded[both, :] = result.astype(jnp.bfloat16)
            square[both, :] = (result * result).astype(jnp.bfloat16)
    for j in range(OWN):
        outbox2[pl.ds(j, WIDE, stride=PAD), :] = interact(pl.ds(j * WIDE, WIDE))

    def send_back(pz, some):
        for base, _ in some:
            peer = base + pz * 4
            pltpu.make_async_remote_copy(
                src_ref=outbox2.at[pl.ds(pl.multiple_of(peer * PAD, PAD), OWN)],
                dst_ref=inbox2.at[my_tile],
                send_sem=send_sem2,
                recv_sem=recv_sem2,
                device_id={"slab": slab, "wide": peer},
                device_id_type=MESH,
            ).start()

    def round_of(favoured, others, own_favoured, own_others):
        def turns(turn, carry):
            pz = lax.rem(z + distance(turn), 16)
            if favoured:

                @pl.when(pz < FIRST)
                def _():
                    send_back(pz, favoured)

            if others:

                @pl.when(pz >= FIRST)
                def _():
                    send_back(pz, others)

            return carry

        lax.fori_loop(0, 15, turns, 0)
        if own_favoured:

            @pl.when(z < FIRST)
            def _():
                send_back(z, own_favoured)

        if own_others:

            @pl.when(z >= FIRST)
            def _():
                send_back(z, own_others)

    round_of(places[:4], (), places[1:4], ())
    round_of(places[4:], places[:4], places[4:], places[1:4])
    round_of((), places[4:], (), places[4:])
    pltpu.make_async_copy(outbox2.at[mine], inbox2.at[my_tile], recv_sem2).start()
    pltpu.make_async_copy(spectrum, spectrum, recv_sem2).wait()

    for sem in (send_sem, send_sem2):
        most = plane.at[pl.ds(0, OWN - 1), pl.ds(0, ROWS)]
        pltpu.make_async_copy(most, most, sem).wait()
        rest = plane.at[0, pl.ds(0, ROWS - OWN)]
        pltpu.make_async_copy(rest, rest, sem).wait()


def unpack_kernel(results, out):
    block = lax.broadcasted_iota(jnp.int32, (8, 128), 1) // TILE

    def unpack(j, carry):
        for h in range(2):
            parts = [results[pl.ds(h * 128 + k * PAD + j, 8, stride=256), :] for k in range(8)]
            for k, part in enumerate(swap_blocks(parts, block)):
                out[j, pl.ds(8 * h + k, 8, stride=16), :] = part
        return carry

    lax.fori_loop(0, OWN, unpack, 0)


def body(spectrum, sea_mask, courant, slot_owner, coupling):
    vmem = pl.BlockSpec(memory_space=pltpu.VMEM)
    anywhere = pl.BlockSpec(memory_space=pltpu.HBM)
    f32, bf16, dma = jnp.float32, jnp.bfloat16, pltpu.SemaphoreType.DMA
    mailbox = pltpu.VMEM((WIDE * PAD, 128), f32)
    square_table = pltpu.VMEM((SLOTS, SLOTS), bf16)
    column = pltpu.VMEM((SLOTS, 128), f32)
    results = pl.pallas_call(
        kernel,
        out_shape=jax.ShapeDtypeStruct((WIDE * PAD, 128), f32),
        in_specs=[anywhere] * 5,
        out_specs=anywhere,
        scratch_shapes=[
            pltpu.VMEM((ROWS, 128), jnp.int32),
            pltpu.SMEM((1, NF), f32),
            pltpu.SMEM((OWN, 128), jnp.int32),
            pltpu.VMEM((OWN, 128), jnp.int32),
            pltpu.VMEM((16, 128), f32),
            pltpu.VMEM((5, 16, 128), f32),
            column,
            pltpu.VMEM((OWN, HOLD, 128), f32),
            square_table,
            mailbox,
            mailbox,
            mailbox,
            pltpu.VMEM((2, 16, 128), f32),
            pltpu.VMEM((2, 16, 128), f32),
            square_table,
            square_table,
            square_table,
            square_table,
            square_table,
            column,
            column,
            column,
            column,
            pltpu.VMEM((SLOTS, 128), bf16),
            pltpu.VMEM((SLOTS, 128), bf16),
            column,
            pltpu.VMEM((2, GROUP, 128), f32),
            pltpu.VMEM((2, GROUP, 128), f32),
            pltpu.VMEM((2, HALF, 128), f32),
            pltpu.VMEM((2, HALF, 128), f32),
            dma,
            dma,
            dma((3,)),
            dma,
            dma,
            dma,
            dma,
            dma,
            dma((2,)),
            dma((2,)),
            dma((4,)),
            dma((4,)),
        ],
        compiler_params=pltpu.CompilerParams(
            collective_id=0, has_side_effects=True, vmem_limit_bytes=60 << 20
        ),
    )(spectrum, sea_mask, courant.reshape(1, NF), slot_owner.reshape(OWN, 128), coupling)
    return pl.pallas_call(
        unpack_kernel,
        out_shape=jax.ShapeDtypeStruct((OWN, ROWS, 128), f32),
        in_specs=[vmem],
        out_specs=vmem,
        compiler_params=pltpu.CompilerParams(vmem_limit_bytes=16 << 20),
    )(results)


def solution(mesh):
    return jax.shard_map(
        body,
        mesh=mesh,
        in_specs=(P("wide", "slab", None), P("slab", None), P(), P(), P()),
        out_specs=P("wide", "slab", None),
        check_vma=False,
    )
```

```python
import math

import jax
import jax.numpy as jnp
from jax import lax
from jax.experimental import pallas as pl
from jax.experimental.pallas import tpu as pltpu
from jax.sharding import PartitionSpec as P

ND = 36
NF = 32
WIDE = 128
OWN = 9
PAD = 16
SLOTS = OWN * WIDE
ROWS = 128
HOLD = 144
TOP = 8
TILE = 16
GROUP = 144
HALF = 72
EARLY = 5
FIRST = 4
MESH = pl.DeviceIdType.MESH

time_step = 0.5


def place(me):
    return me // 64, (me // 4) % 16, me % 4


def tile_of(y, x):
    return jnp.where(y == 0, x, 7 - x)


def device_of(z, q):
    y = q // 4
    return y * 64 + z * 4 + jnp.where(y == 0, q, 7 - q)


def distance(turn):
    far = 8 - (turn + 1) // 2
    return lax.rem(jnp.where(lax.rem(turn, 2) == 1, far, 16 - far), 16)


def swap_blocks(parts, block):
    parts = list(parts)
    for bit in (4, 2, 1):
        high = (block & bit) != 0
        for a in range(8):
            if a & bit:
                continue
            first, second = parts[a], parts[a + bit]
            parts[a] = jnp.where(high, pltpu.roll(second, TILE * bit, 1), first)
            parts[a + bit] = jnp.where(high, second, pltpu.roll(first, 128 - TILE * bit, 1))
    return parts


def kernel(
    spectrum,
    sea_hbm,
    courant_hbm,
    owner_hbm,
    coupling,
    inbox2,
    sea_mask,
    courant,
    owner_scalar,
    owner_rows,
    owner,
    own_speed,
    natural,
    plane,
    table_in,
    outbox,
    inbox,
    outbox2,
    rim_out,
    rim_in,
    picker,
    picker_t,
    half_table,
    table,
    table_t,
    owner_wide,
    east_wide,
    north_wide,
    moved,
    rounded,
    square,
    energy,
    row_out,
    row_in,
    col_out,
    col_in,
    load_sem,
    sea_sem,
    small_sem,
    table_sem,
    send_sem,
    recv_sem,
    send_sem2,
    recv_sem2,
    rim_send,
    rim_recv,
    edge_send,
    edge_recv,
):
    slab = lax.axis_index("slab")
    me = lax.axis_index("wide")
    y, z, x = place(me)
    q = tile_of(y, x)
    spot = z * 8 + q
    places = []
    for p in range(8):
        py, px = lax.rem(y + p // 4, 2), lax.rem(x + p % 4, 4)
        places.append((py * 64 + px, tile_of(py, px)))
    up_slab, down_slab = (slab + 1) % 4, (slab + 3) % 4
    north_id = {
        "slab": jnp.where(z == 15, up_slab, slab),
        "wide": y * 64 + ((z + 1) % 16) * 4 + x,
    }
    south_id = {
        "slab": jnp.where(z == 0, down_slab, slab),
        "wide": y * 64 + ((z + 15) % 16) * 4 + x,
    }
    east_id = {"slab": slab, "wide": device_of(z, (q + 1) % 8)}
    west_id = {"slab": slab, "wide": device_of(z, (q + 7) % 8)}

    small_loads = [
        pltpu.make_async_copy(owner_hbm, owner_scalar, small_sem.at[0]),
        pltpu.make_async_copy(courant_hbm, courant, small_sem.at[1]),
        pltpu.make_async_copy(owner_hbm, owner_rows, small_sem.at[2]),
    ]
    sea_load = pltpu.make_async_copy(sea_hbm, sea_mask, sea_sem)
    for load in (*small_loads, sea_load):
        load.start()
    loads = pltpu.make_async_copy(spectrum, plane.at[:, pl.ds(TOP, ROWS)], load_sem)
    loads.start()
    table_load = pltpu.make_async_copy(coupling, table_in, table_sem)
    table_load.start()

    barrier = pltpu.get_barrier_semaphore()
    for there in (
        {"slab": up_slab, "wide": me},
        {"slab": down_slab, "wide": me},
        north_id,
        south_id,
    ):
        pl.semaphore_signal(barrier, inc=1, device_id=there, device_id_type=MESH)

    def greet(turn, first=0):
        pz = lax.rem(z + distance(turn), 16) if first == 0 else z
        for base, _ in places[first:]:
            pl.semaphore_signal(
                barrier, inc=1, device_id={"slab": slab, "wide": base + pz * 4}, device_id_type=MESH
            )

    for turn in (0, 1, 2, 3, 13, 14):
        greet(turn)
    greet(0, 1)
    for load in small_loads:
        load.wait()
    row16 = lax.broadcasted_iota(jnp.int32, (16, 128), 0)
    own_angle = jnp.zeros((16, 128), jnp.float32)
    own_courant = jnp.zeros((16, 128), jnp.float32)
    for j in range(OWN):
        slot = me * OWN + j
        component = owner_scalar[slot // 128, slot % 128]
        freq = component // ND
        angle = (component - freq * ND).astype(jnp.float32) * (2.0 * math.pi / ND)
        own_angle = jnp.where(row16 == j, angle, own_angle)
        own_courant = jnp.where(row16 == j, courant[0, freq], own_courant)
    east, north = own_courant * jnp.cos(own_angle), own_courant * jnp.sin(own_angle)
    own_speed[0] = 1.0 - jnp.abs(east) - jnp.abs(north)
    own_speed[1] = jnp.maximum(east, 0.0)
    own_speed[2] = jnp.maximum(-east, 0.0)
    own_speed[3] = jnp.maximum(north, 0.0)
    own_speed[4] = jnp.maximum(-north, 0.0)

    lane = lax.broadcasted_iota(jnp.int32, (8, 128), 1)
    block = lane // TILE

    sea_load.wait()
    loads.wait()
    sea = sea_mask[...].astype(jnp.float32)
    for j in range(OWN):
        plane[j, pl.ds(TOP, ROWS), :] = plane[j, pl.ds(TOP, ROWS), :] * sea
        plane[j, pl.ds(TOP - 8, 8), :] = jnp.zeros((8, 128), jnp.float32)
        plane[j, pl.ds(TOP + ROWS, 8), :] = jnp.zeros((8, 128), jnp.float32)
        rim_out[0, pl.ds(j, 1), :] = own_speed[3, pl.ds(j, 1), :] * plane[j, pl.ds(TOP + ROWS - 1, 1), :]
        rim_out[1, pl.ds(j, 1), :] = own_speed[4, pl.ds(j, 1), :] * plane[j, pl.ds(TOP, 1), :]

    def propagate(j, carry):
        greet(j + 4)
        remain, east, west, north, south = [own_speed[u, pl.ds(j, 1), :] for u in range(5)]
        for h in range(2):
            parts = []
            for k in range(8):
                start = TOP + 8 * h + k
                here = plane[j, pl.ds(start, 8, stride=16), :]
                part = remain * here + east * pltpu.roll(here, 1, 1)
                part = part + west * pltpu.roll(here, 127, 1)
                part = part + north * plane[j, pl.ds(start - 1, 8, stride=16), :]
                parts.append(part + south * plane[j, pl.ds(start + 1, 8, stride=16), :])
            for k, part in enumerate(swap_blocks(parts, block)):
                outbox[pl.ds(h * 128 + k * PAD + j, 8, stride=256), :] = part
        return carry

    lax.fori_loop(0, OWN, propagate, 0, unroll=3)

    pl.semaphore_wait(barrier, WIDE - 1 + 4)

    rims = []
    for side, there in ((0, up_slab), (1, down_slab)):
        rims.append(
            pltpu.make_async_remote_copy(
                src_ref=rim_out.at[side, pl.ds(0, OWN)],
                dst_ref=rim_in.at[side, pl.ds(0, OWN)],
                send_sem=rim_send.at[side],
                recv_sem=rim_recv.at[side],
                device_id={"slab": there, "wide": me},
                device_id_type=MESH,
            )
        )
        rims[-1].start()
    mine = pl.ds(pl.multiple_of(me * PAD, PAD), OWN)
    my_tile = pl.ds(pl.multiple_of(spot * PAD, PAD), OWN)

    def send(pz, first=0):
        for base, tile in places[first:]:
            pltpu.make_async_remote_copy(
                src_ref=outbox.at[pl.ds(pl.multiple_of((pz * 8 + tile) * PAD, PAD), OWN)],
                dst_ref=inbox.at[mine],
                send_sem=send_sem,
                recv_sem=recv_sem,
                device_id={"slab": slab, "wide": base + pz * 4},
                device_id_type=MESH,
            ).start()

    def send_inner(turn, carry):
        pz = lax.rem(z + distance(turn), 16)

        @pl.when(jnp.logical_and(pz > 0, pz < 15))
        def _():
            send(pz)

        return carry

    def send_outer(turn, carry):
        pz = lax.rem(z + distance(turn), 16)

        @pl.when(jnp.logical_or(pz == 0, pz == 15))
        def _():
            send(pz)

        return carry

    def send_any(turn, carry):
        send(lax.rem(z + distance(turn), 16))
        return carry

    lax.fori_loop(0, EARLY, send_inner, 0)
    for rim in rims:
        rim.wait()
    lane9 = lax.broadcasted_iota(jnp.int32, (OWN, 128), 1)
    below = jnp.where(slab > 0, 1.0, 0.0) * rim_in[0, pl.ds(0, OWN), :]
    above = jnp.where(slab < 3, 1.0, 0.0) * rim_in[1, pl.ds(0, OWN), :]
    for k in range(8):
        low = pltpu.roll(below, (128 - TILE * k) % 128, 1) if k else below
        rows = pl.ds(k * PAD, OWN)
        outbox[rows, :] = outbox[rows, :] + jnp.where(lane9 < TILE, low, 0.0)
        high = pltpu.roll(above, 112 - TILE * k, 1) if k < 7 else above
        rows = pl.ds((15 * 8 + k) * PAD, OWN)
        outbox[rows, :] = outbox[rows, :] + jnp.where(lane9 >= 112, high, 0.0)
    lax.fori_loop(0, EARLY, send_outer, 0)
    lax.fori_loop(EARLY, 15, send_any, 0)
    send(z, 1)
    pltpu.make_async_copy(outbox.at[my_tile], inbox.at[mine], recv_sem).start()

    owners = owner_rows[...].astype(jnp.float32)
    band = jnp.floor((owners + 0.5) * (1.0 / ND))
    angle = (owners - band * ND) * (2.0 * math.pi / ND)
    speed = jnp.zeros((OWN, 128), jnp.float32)
    for f in range(NF):
        speed = jnp.where(band == f, courant[0, f], speed)
    wide_rows = (owners, speed * jnp.cos(angle), speed * jnp.sin(angle))
    for wide_form, row_form in zip((owner_wide, east_wide, north_wide), wide_rows):
        for j in range(OWN):
            natural[pl.ds(j * 128, 128), :] = jnp.broadcast_to(row_form[j : j + 1], (128, 128)).T
        for j in range(OWN):
            wide_form[pl.ds(j * WIDE, WIDE), :] = natural[pl.ds(j, WIDE, stride=OWN), :]
    for j in range(OWN):
        owner[pl.ds(j, 1), :] = owner_wide[pl.ds(j * WIDE, WIDE), :].T[0:1]

    lanes = lax.broadcasted_iota(jnp.int32, (128, 128), 1).astype(jnp.float32)
    sublanes = lax.broadcasted_iota(jnp.int32, (128, 128), 0).astype(jnp.float32)

    def pick(i, carry):
        rows = pl.ds(pl.multiple_of(i * 128, 128), 128)
        base = (i * 128).astype(jnp.float32)
        for j in range(OWN):
            columns = pl.ds(j * 128, 128)
            hit = owner_wide[rows, :] == lanes + 128.0 * j
            picker[rows, columns] = jnp.where(hit, 1.0, 0.0).astype(jnp.bfloat16)
            hit = owner[pl.ds(j, 1), :] == sublanes + base
            picker_t[rows, columns] = jnp.where(hit, 1.0, 0.0).astype(jnp.bfloat16)
        return carry

    lax.fori_loop(0, OWN, pick, 0)
    table_load.wait()

    def rows_picked(i, carry):
        rows = pl.ds(pl.multiple_of(i * 128, 128), 128)
        half_table[rows, :] = jnp.dot(
            picker[rows, :], table_in[...], preferred_element_type=jnp.float32
        ).astype(jnp.bfloat16)
        return carry

    lax.fori_loop(0, OWN, rows_picked, 0)

    def columns_picked(i, carry):
        rows = pl.ds(pl.multiple_of(i * 128, 128), 128)
        full = jnp.dot(half_table[rows, :], picker_t[...], preferred_element_type=jnp.float32)
        table[rows, :] = full.astype(jnp.bfloat16)
        for j in range(OWN):
            table_t[pl.ds(j * 128, 128), rows] = full[:, j * 128 : (j + 1) * 128].T.astype(jnp.bfloat16)
        return carry

    lax.fori_loop(0, OWN, columns_picked, 0)

    tile_sea = sea_mask[pl.ds(pl.multiple_of(z * 8, 8), 8), :].astype(jnp.float32)
    column = lax.broadcasted_iota(jnp.int32, (128, 128), 0)
    target = lax.broadcasted_iota(jnp.int32, (128, 128), 1)
    spread = jnp.where(column == q * TILE + target % TILE, 1.0, 0.0)
    tile_sea = jnp.dot(tile_sea, spread, preferred_element_type=jnp.float32)
    inner = lax.broadcasted_iota(jnp.int32, (8, 128), 0)
    tile_sea = jnp.sum(jnp.where(inner == block, tile_sea, 0.0), axis=0, keepdims=True)

    pltpu.make_async_copy(spectrum, spectrum, recv_sem).wait()
    for j in range(OWN):
        rows = pl.ds(j * WIDE, WIDE)
        value = inbox[pl.ds(j, WIDE, stride=PAD), :]
        moved[rows, :] = value
        rounded[rows, :] = value.astype(jnp.bfloat16)
        square[rows, :] = (value * value).astype(jnp.bfloat16)

    def interact(rows):
        value = moved[rows, :]
        gain = value * jnp.dot(table[rows, :], rounded[...], preferred_element_type=jnp.float32)
        loss = jnp.dot(table_t[rows, :], square[...], preferred_element_type=jnp.float32)
        return tile_sea * jnp.maximum(value + time_step * (gain - loss), 0.0)

    lane_g = lax.broadcasted_iota(jnp.int32, (GROUP, 128), 1)
    lane_h = lax.broadcasted_iota(jnp.int32, (HALF, 128), 1)
    for g in range(8):
        rows = pl.ds(g * GROUP, GROUP)
        value = interact(rows)
        energy[rows, :] = value
        north = pltpu.roll(value, (TILE * (g + 1)) % 128, 1) if g < 7 else value
        south = pltpu.roll(value, TILE * g, 1) if g else value
        here = lane_g // TILE == g
        if g:
            north = jnp.where(here, north, row_out[0])
            south = jnp.where(here, south, row_out[1])
        row_out[0] = north
        row_out[1] = south
        for u in range(2):
            b = 2 * g + u
            part = value[u * HALF : (u + 1) * HALF]
            east = pltpu.roll(part, (b + 113) % 128, 1) if b != 15 else part
            west = pltpu.roll(part, b, 1) if b else part
            here = lane_h % TILE == b
            if b:
                east = jnp.where(here, east, col_out[0])
                west = jnp.where(here, west, col_out[1])
            col_out[0] = east
            col_out[1] = west

    edges = []
    for e, (source, sink, side, there) in enumerate(
        (
            (row_out, row_in, 0, north_id),
            (row_out, row_in, 1, south_id),
            (col_out, col_in, 0, east_id),
            (col_out, col_in, 1, west_id),
        )
    ):
        edges.append(
            pltpu.make_async_remote_copy(
                src_ref=source.at[side],
                dst_ref=sink.at[side],
                send_sem=edge_send.at[e],
                recv_sem=edge_recv.at[e],
                device_id=there,
                device_id_type=MESH,
            )
        )
        edges[-1].start()
    for b in range(16):
        rows = pl.ds(b * HALF, HALF)
        value = energy[rows, :]
        west = jnp.where(lane_h % TILE == 0, 0.0, pltpu.roll(value, 1, 1))
        east = jnp.where(lane_h % TILE == TILE - 1, 0.0, pltpu.roll(value, 127, 1))
        south = jnp.where(lane_h < TILE, 0.0, pltpu.roll(value, TILE, 1))
        north = jnp.where(lane_h >= 112, 0.0, pltpu.roll(value, 112, 1))
        e, n = east_wide[rows, :], north_wide[rows, :]
        result = (1.0 - jnp.abs(e) - jnp.abs(n)) * value + jnp.maximum(e, 0.0) * west
        result = result + jnp.maximum(-e, 0.0) * east
        result = result + jnp.maximum(n, 0.0) * south
        moved[rows, :] = result + jnp.maximum(-n, 0.0) * north

    for edge in edges:
        edge.wait()

    has_south = jnp.logical_or(slab > 0, z > 0)
    has_north = jnp.logical_or(slab < 3, z < 15)
    keep_south = jnp.where(has_south, 1.0, 0.0)
    keep_north = jnp.where(has_north, 1.0, 0.0)
    for b in range(16):
        g, u = b // 2, b % 2
        rows = pl.ds(b * HALF, HALF)
        packed = pl.ds(u * HALF, HALF)
        west, east = col_in[0], col_in[1]
        west = pltpu.roll(west, 128 - b, 1) if b else west
        east = pltpu.roll(east, 15 - b, 1) if b != 15 else east
        south = keep_south * row_in[0, packed, :]
        south = pltpu.roll(south, 128 - TILE * g, 1) if g else south
        north = keep_north * row_in[1, packed, :]
        north = pltpu.roll(north, 112 - TILE * g, 1) if g < 7 else north
        e, n = east_wide[rows, :], north_wide[rows, :]
        result = moved[rows, :]
        result = result + jnp.where(lane_h % TILE == 0, jnp.maximum(e, 0.0) * west, 0.0)
        result = result + jnp.where(lane_h % TILE == TILE - 1, jnp.maximum(-e, 0.0) * east, 0.0)
        result = result + jnp.where(lane_h < TILE, jnp.maximum(n, 0.0) * south, 0.0)
        result = result + jnp.where(lane_h >= 112, jnp.maximum(-n, 0.0) * north, 0.0)
        moved[rows, :] = result
        if u:
            both = pl.ds(g * GROUP, GROUP)
            result = moved[both, :]
            rounded[both, :] = result.astype(jnp.bfloat16)
            square[both, :] = (result * result).astype(jnp.bfloat16)
    for j in range(OWN):
        outbox2[pl.ds(j, WIDE, stride=PAD), :] = interact(pl.ds(j * WIDE, WIDE))

    def send_back(pz, some):
        for base, _ in some:
            peer = base + pz * 4
            pltpu.make_async_remote_copy(
                src_ref=outbox2.at[pl.ds(pl.multiple_of(peer * PAD, PAD), OWN)],
                dst_ref=inbox2.at[my_tile],
                send_sem=send_sem2,
                recv_sem=recv_sem2,
                device_id={"slab": slab, "wide": peer},
                device_id_type=MESH,
            ).start()

    def round_of(favoured, others, own_favoured, own_others):
        def turns(turn, carry):
            pz = lax.rem(z + distance(turn), 16)
            if favoured:

                @pl.when(pz < FIRST)
                def _():
                    send_back(pz, favoured)

            if others:

                @pl.when(pz >= FIRST)
                def _():
                    send_back(pz, others)

            return carry

        lax.fori_loop(0, 15, turns, 0)
        if own_favoured:

            @pl.when(z < FIRST)
            def _():
                send_back(z, own_favoured)

        if own_others:

            @pl.when(z >= FIRST)
            def _():
                send_back(z, own_others)

    round_of(places[:4], (), places[1:4], ())
    round_of(places[4:], places[:4], places[4:], places[1:4])
    round_of((), places[4:], (), places[4:])
    pltpu.make_async_copy(outbox2.at[mine], inbox2.at[my_tile], recv_sem2).start()
    pltpu.make_async_copy(spectrum, spectrum, recv_sem2).wait()

    for sem in (send_sem, send_sem2):
        most = plane.at[pl.ds(0, OWN - 1), pl.ds(0, ROWS)]
        pltpu.make_async_copy(most, most, sem).wait()
        rest = plane.at[0, pl.ds(0, ROWS - OWN)]
        pltpu.make_async_copy(rest, rest, sem).wait()


def unpack_kernel(results, out):
    block = lax.broadcasted_iota(jnp.int32, (8, 128), 1) // TILE

    def unpack(j, carry):
        for h in range(2):
            parts = [results[pl.ds(h * 128 + k * PAD + j, 8, stride=256), :] for k in range(8)]
            for k, part in enumerate(swap_blocks(parts, block)):
                out[j, pl.ds(8 * h + k, 8, stride=16), :] = part
        return carry

    lax.fori_loop(0, OWN, unpack, 0, unroll=3)


def body(spectrum, sea_mask, courant, slot_owner, coupling):
    vmem = pl.BlockSpec(memory_space=pltpu.VMEM)
    anywhere = pl.BlockSpec(memory_space=pltpu.HBM)
    f32, bf16, dma = jnp.float32, jnp.bfloat16, pltpu.SemaphoreType.DMA
    mailbox = pltpu.VMEM((WIDE * PAD, 128), f32)
    square_table = pltpu.VMEM((SLOTS, SLOTS), bf16)
    column = pltpu.VMEM((SLOTS, 128), f32)
    results = pl.pallas_call(
        kernel,
        out_shape=jax.ShapeDtypeStruct((WIDE * PAD, 128), f32),
        in_specs=[anywhere] * 5,
        out_specs=anywhere,
        scratch_shapes=[
            pltpu.VMEM((ROWS, 128), jnp.int32),
            pltpu.SMEM((1, NF), f32),
            pltpu.SMEM((OWN, 128), jnp.int32),
            pltpu.VMEM((OWN, 128), jnp.int32),
            pltpu.VMEM((16, 128), f32),
            pltpu.VMEM((5, 16, 128), f32),
            column,
            pltpu.VMEM((OWN, HOLD, 128), f32),
            square_table,
            mailbox,
            mailbox,
            mailbox,
            pltpu.VMEM((2, 16, 128), f32),
            pltpu.VMEM((2, 16, 128), f32),
            square_table,
            square_table,
            square_table,
            square_table,
            square_table,
            column,
            column,
            column,
            column,
            pltpu.VMEM((SLOTS, 128), bf16),
            pltpu.VMEM((SLOTS, 128), bf16),
            column,
            pltpu.VMEM((2, GROUP, 128), f32),
            pltpu.VMEM((2, GROUP, 128), f32),
            pltpu.VMEM((2, HALF, 128), f32),
            pltpu.VMEM((2, HALF, 128), f32),
            dma,
            dma,
            dma((3,)),
            dma,
            dma,
            dma,
            dma,
            dma,
            dma((2,)),
            dma((2,)),
            dma((4,)),
            dma((4,)),
        ],
        compiler_params=pltpu.CompilerParams(
            collective_id=0, has_side_effects=True, vmem_limit_bytes=60 << 20
        ),
    )(spectrum, sea_mask, courant.reshape(1, NF), slot_owner.reshape(OWN, 128), coupling)
    return pl.pallas_call(
        unpack_kernel,
        out_shape=jax.ShapeDtypeStruct((OWN, ROWS, 128), f32),
        in_specs=[vmem],
        out_specs=vmem,
        compiler_params=pltpu.CompilerParams(vmem_limit_bytes=16 << 20),
    )(results)


def solution(mesh):
    return jax.shard_map(
        body,
        mesh=mesh,
        in_specs=(P("wide", "slab", None), P("slab", None), P(), P(), P()),
        out_specs=P("wide", "slab", None),
        check_vma=False,
    )
```

```python
import math

import jax
import jax.numpy as jnp
from jax import lax
from jax.experimental import pallas as pl
from jax.experimental.pallas import tpu as pltpu
from jax.sharding import PartitionSpec as P

ND = 36
NF = 32
WIDE = 128
OWN = 9
PAD = 16
SLOTS = OWN * WIDE
ROWS = 128
HOLD = 144
TOP = 8
TILE = 16
GROUP = 144
HALF = 72
EARLY = 5
FIRST, SECOND = 2, 6
MESH = pl.DeviceIdType.MESH

time_step = 0.5


def place(me):
    return me // 64, (me // 4) % 16, me % 4


def tile_of(y, x):
    return jnp.where(y == 0, x, 7 - x)


def device_of(z, q):
    y = q // 4
    return y * 64 + z * 4 + jnp.where(y == 0, q, 7 - q)


def distance(turn):
    far = 8 - (turn + 1) // 2
    return lax.rem(jnp.where(lax.rem(turn, 2) == 1, far, 16 - far), 16)


def swap_blocks(parts, block):
    parts = list(parts)
    for bit in (4, 2, 1):
        high = (block & bit) != 0
        for a in range(8):
            if a & bit:
                continue
            first, second = parts[a], parts[a + bit]
            parts[a] = jnp.where(high, pltpu.roll(second, TILE * bit, 1), first)
            parts[a + bit] = jnp.where(high, second, pltpu.roll(first, 128 - TILE * bit, 1))
    return parts


def kernel(
    spectrum,
    sea_hbm,
    courant_hbm,
    owner_hbm,
    coupling,
    inbox2,
    sea_mask,
    courant,
    owner_scalar,
    owner_rows,
    owner,
    own_speed,
    natural,
    plane,
    table_in,
    outbox,
    inbox,
    outbox2,
    rim_out,
    rim_in,
    picker,
    picker_t,
    half_table,
    table,
    table_t,
    owner_wide,
    east_wide,
    north_wide,
    moved,
    rounded,
    square,
    energy,
    row_out,
    row_in,
    col_out,
    col_in,
    load_sem,
    sea_sem,
    small_sem,
    table_sem,
    send_sem,
    recv_sem,
    send_sem2,
    recv_sem2,
    rim_send,
    rim_recv,
    edge_send,
    edge_recv,
):
    slab = lax.axis_index("slab")
    me = lax.axis_index("wide")
    y, z, x = place(me)
    q = tile_of(y, x)
    spot = z * 8 + q
    places = []
    for p in range(8):
        py, px = lax.rem(y + p // 4, 2), lax.rem(x + p % 4, 4)
        places.append((py * 64 + px, tile_of(py, px)))
    up_slab, down_slab = (slab + 1) % 4, (slab + 3) % 4
    north_id = {
        "slab": jnp.where(z == 15, up_slab, slab),
        "wide": y * 64 + ((z + 1) % 16) * 4 + x,
    }
    south_id = {
        "slab": jnp.where(z == 0, down_slab, slab),
        "wide": y * 64 + ((z + 15) % 16) * 4 + x,
    }
    east_id = {"slab": slab, "wide": device_of(z, (q + 1) % 8)}
    west_id = {"slab": slab, "wide": device_of(z, (q + 7) % 8)}

    small_loads = [
        pltpu.make_async_copy(owner_hbm, owner_scalar, small_sem.at[0]),
        pltpu.make_async_copy(courant_hbm, courant, small_sem.at[1]),
        pltpu.make_async_copy(owner_hbm, owner_rows, small_sem.at[2]),
    ]
    sea_load = pltpu.make_async_copy(sea_hbm, sea_mask, sea_sem)
    for load in (*small_loads, sea_load):
        load.start()
    loads = pltpu.make_async_copy(spectrum, plane.at[:, pl.ds(TOP, ROWS)], load_sem)
    loads.start()
    table_load = pltpu.make_async_copy(coupling, table_in, table_sem)
    table_load.start()

    barrier = pltpu.get_barrier_semaphore()
    for there in (
        {"slab": up_slab, "wide": me},
        {"slab": down_slab, "wide": me},
        north_id,
        south_id,
    ):
        pl.semaphore_signal(barrier, inc=1, device_id=there, device_id_type=MESH)

    def greet(turn, first=0):
        pz = lax.rem(z + distance(turn), 16) if first == 0 else z
        for base, _ in places[first:]:
            pl.semaphore_signal(
                barrier, inc=1, device_id={"slab": slab, "wide": base + pz * 4}, device_id_type=MESH
            )

    for turn in (0, 1, 2, 3, 13, 14):
        greet(turn)
    greet(0, 1)
    for load in small_loads:
        load.wait()
    row16 = lax.broadcasted_iota(jnp.int32, (16, 128), 0)
    own_angle = jnp.zeros((16, 128), jnp.float32)
    own_courant = jnp.zeros((16, 128), jnp.float32)
    for j in range(OWN):
        slot = me * OWN + j
        component = owner_scalar[slot // 128, slot % 128]
        freq = component // ND
        angle = (component - freq * ND).astype(jnp.float32) * (2.0 * math.pi / ND)
        own_angle = jnp.where(row16 == j, angle, own_angle)
        own_courant = jnp.where(row16 == j, courant[0, freq], own_courant)
    east, north = own_courant * jnp.cos(own_angle), own_courant * jnp.sin(own_angle)
    own_speed[0] = 1.0 - jnp.abs(east) - jnp.abs(north)
    own_speed[1] = jnp.maximum(east, 0.0)
    own_speed[2] = jnp.maximum(-east, 0.0)
    own_speed[3] = jnp.maximum(north, 0.0)
    own_speed[4] = jnp.maximum(-north, 0.0)

    lane = lax.broadcasted_iota(jnp.int32, (8, 128), 1)
    block = lane // TILE

    sea_load.wait()
    loads.wait()
    sea = sea_mask[...].astype(jnp.float32)
    for j in range(OWN):
        plane[j, pl.ds(TOP, ROWS), :] = plane[j, pl.ds(TOP, ROWS), :] * sea
        plane[j, pl.ds(TOP - 8, 8), :] = jnp.zeros((8, 128), jnp.float32)
        plane[j, pl.ds(TOP + ROWS, 8), :] = jnp.zeros((8, 128), jnp.float32)
        rim_out[0, pl.ds(j, 1), :] = own_speed[3, pl.ds(j, 1), :] * plane[j, pl.ds(TOP + ROWS - 1, 1), :]
        rim_out[1, pl.ds(j, 1), :] = own_speed[4, pl.ds(j, 1), :] * plane[j, pl.ds(TOP, 1), :]

    def propagate(j, carry):
        greet(j + 4)
        remain, east, west, north, south = [own_speed[u, pl.ds(j, 1), :] for u in range(5)]
        for h in range(2):
            parts = []
            for k in range(8):
                start = TOP + 8 * h + k
                here = plane[j, pl.ds(start, 8, stride=16), :]
                part = remain * here + east * pltpu.roll(here, 1, 1)
                part = part + west * pltpu.roll(here, 127, 1)
                part = part + north * plane[j, pl.ds(start - 1, 8, stride=16), :]
                parts.append(part + south * plane[j, pl.ds(start + 1, 8, stride=16), :])
            for k, part in enumerate(swap_blocks(parts, block)):
                outbox[pl.ds(h * 128 + k * PAD + j, 8, stride=256), :] = part
        return carry

    lax.fori_loop(0, OWN, propagate, 0, unroll=3)

    pl.semaphore_wait(barrier, WIDE - 1 + 4)

    rims = []
    for side, there in ((0, up_slab), (1, down_slab)):
        rims.append(
            pltpu.make_async_remote_copy(
                src_ref=rim_out.at[side, pl.ds(0, OWN)],
                dst_ref=rim_in.at[side, pl.ds(0, OWN)],
                send_sem=rim_send.at[side],
                recv_sem=rim_recv.at[side],
                device_id={"slab": there, "wide": me},
                device_id_type=MESH,
            )
        )
        rims[-1].start()
    mine = pl.ds(pl.multiple_of(me * PAD, PAD), OWN)
    my_tile = pl.ds(pl.multiple_of(spot * PAD, PAD), OWN)

    def send(pz, first=0):
        for base, tile in places[first:]:
            pltpu.make_async_remote_copy(
                src_ref=outbox.at[pl.ds(pl.multiple_of((pz * 8 + tile) * PAD, PAD), OWN)],
                dst_ref=inbox.at[mine],
                send_sem=send_sem,
                recv_sem=recv_sem,
                device_id={"slab": slab, "wide": base + pz * 4},
                device_id_type=MESH,
            ).start()

    def send_inner(turn, carry):
        pz = lax.rem(z + distance(turn), 16)

        @pl.when(jnp.logical_and(pz > 0, pz < 15))
        def _():
            send(pz)

        return carry

    def send_outer(turn, carry):
        pz = lax.rem(z + distance(turn), 16)

        @pl.when(jnp.logical_or(pz == 0, pz == 15))
        def _():
            send(pz)

        return carry

    def send_any(turn, carry):
        send(lax.rem(z + distance(turn), 16))
        return carry

    lax.fori_loop(0, EARLY, send_inner, 0)
    for rim in rims:
        rim.wait()
    lane9 = lax.broadcasted_iota(jnp.int32, (OWN, 128), 1)
    below = jnp.where(slab > 0, 1.0, 0.0) * rim_in[0, pl.ds(0, OWN), :]
    above = jnp.where(slab < 3, 1.0, 0.0) * rim_in[1, pl.ds(0, OWN), :]
    for k in range(8):
        low = pltpu.roll(below, (128 - TILE * k) % 128, 1) if k else below
        rows = pl.ds(k * PAD, OWN)
        outbox[rows, :] = outbox[rows, :] + jnp.where(lane9 < TILE, low, 0.0)
        high = pltpu.roll(above, 112 - TILE * k, 1) if k < 7 else above
        rows = pl.ds((15 * 8 + k) * PAD, OWN)
        outbox[rows, :] = outbox[rows, :] + jnp.where(lane9 >= 112, high, 0.0)
    lax.fori_loop(0, EARLY, send_outer, 0)
    lax.fori_loop(EARLY, 15, send_any, 0)
    send(z, 1)
    pltpu.make_async_copy(outbox.at[my_tile], inbox.at[mine], recv_sem).start()

    owners = owner_rows[...].astype(jnp.float32)
    band = jnp.floor((owners + 0.5) * (1.0 / ND))
    angle = (owners - band * ND) * (2.0 * math.pi / ND)
    speed = jnp.zeros((OWN, 128), jnp.float32)
    for f in range(NF):
        speed = jnp.where(band == f, courant[0, f], speed)
    wide_rows = (owners, speed * jnp.cos(angle), speed * jnp.sin(angle))
    for wide_form, row_form in zip((owner_wide, east_wide, north_wide), wide_rows):
        for j in range(OWN):
            natural[pl.ds(j * 128, 128), :] = jnp.broadcast_to(row_form[j : j + 1], (128, 128)).T
        for j in range(OWN):
            wide_form[pl.ds(j * WIDE, WIDE), :] = natural[pl.ds(j, WIDE, stride=OWN), :]
    for j in range(OWN):
        owner[pl.ds(j, 1), :] = owner_wide[pl.ds(j * WIDE, WIDE), :].T[0:1]

    lanes = lax.broadcasted_iota(jnp.int32, (128, 128), 1).astype(jnp.float32)
    sublanes = lax.broadcasted_iota(jnp.int32, (128, 128), 0).astype(jnp.float32)

    def pick(i, carry):
        rows = pl.ds(pl.multiple_of(i * 128, 128), 128)
        base = (i * 128).astype(jnp.float32)
        for j in range(OWN):
            columns = pl.ds(j * 128, 128)
            hit = owner_wide[rows, :] == lanes + 128.0 * j
            picker[rows, columns] = jnp.where(hit, 1.0, 0.0).astype(jnp.bfloat16)
            hit = owner[pl.ds(j, 1), :] == sublanes + base
            picker_t[rows, columns] = jnp.where(hit, 1.0, 0.0).astype(jnp.bfloat16)
        return carry

    lax.fori_loop(0, OWN, pick, 0)
    table_load.wait()

    def rows_picked(i, carry):
        rows = pl.ds(pl.multiple_of(i * 128, 128), 128)
        half_table[rows, :] = jnp.dot(
            picker[rows, :], table_in[...], preferred_element_type=jnp.float32
        ).astype(jnp.bfloat16)
        return carry

    lax.fori_loop(0, OWN, rows_picked, 0)

    def columns_picked(i, carry):
        rows = pl.ds(pl.multiple_of(i * 128, 128), 128)
        full = jnp.dot(half_table[rows, :], picker_t[...], preferred_element_type=jnp.float32)
        table[rows, :] = full.astype(jnp.bfloat16)
        for j in range(OWN):
            table_t[pl.ds(j * 128, 128), rows] = full[:, j * 128 : (j + 1) * 128].T.astype(jnp.bfloat16)
        return carry

    lax.fori_loop(0, OWN, columns_picked, 0)

    tile_sea = sea_mask[pl.ds(pl.multiple_of(z * 8, 8), 8), :].astype(jnp.float32)
    column = lax.broadcasted_iota(jnp.int32, (128, 128), 0)
    target = lax.broadcasted_iota(jnp.int32, (128, 128), 1)
    spread = jnp.where(column == q * TILE + target % TILE, 1.0, 0.0)
    tile_sea = jnp.dot(tile_sea, spread, preferred_element_type=jnp.float32)
    inner = lax.broadcasted_iota(jnp.int32, (8, 128), 0)
    tile_sea = jnp.sum(jnp.where(inner == block, tile_sea, 0.0), axis=0, keepdims=True)

    pltpu.make_async_copy(spectrum, spectrum, recv_sem).wait()
    for j in range(OWN):
        rows = pl.ds(j * WIDE, WIDE)
        value = inbox[pl.ds(j, WIDE, stride=PAD), :]
        moved[rows, :] = value
        rounded[rows, :] = value.astype(jnp.bfloat16)
        square[rows, :] = (value * value).astype(jnp.bfloat16)

    def interact(rows):
        value = moved[rows, :]
        gain = value * jnp.dot(table[rows, :], rounded[...], preferred_element_type=jnp.float32)
        loss = jnp.dot(table_t[rows, :], square[...], preferred_element_type=jnp.float32)
        return tile_sea * jnp.maximum(value + time_step * (gain - loss), 0.0)

    lane_g = lax.broadcasted_iota(jnp.int32, (GROUP, 128), 1)
    lane_h = lax.broadcasted_iota(jnp.int32, (HALF, 128), 1)
    for g in range(8):
        rows = pl.ds(g * GROUP, GROUP)
        value = interact(rows)
        energy[rows, :] = value
        north = pltpu.roll(value, (TILE * (g + 1)) % 128, 1) if g < 7 else value
        south = pltpu.roll(value, TILE * g, 1) if g else value
        here = lane_g // TILE == g
        if g:
            north = jnp.where(here, north, row_out[0])
            south = jnp.where(here, south, row_out[1])
        row_out[0] = north
        row_out[1] = south
        for u in range(2):
            b = 2 * g + u
            part = value[u * HALF : (u + 1) * HALF]
            east = pltpu.roll(part, (b + 113) % 128, 1) if b != 15 else part
            west = pltpu.roll(part, b, 1) if b else part
            here = lane_h % TILE == b
            if b:
                east = jnp.where(here, east, col_out[0])
                west = jnp.where(here, west, col_out[1])
            col_out[0] = east
            col_out[1] = west

    edges = []
    for e, (source, sink, side, there) in enumerate(
        (
            (row_out, row_in, 0, north_id),
            (row_out, row_in, 1, south_id),
            (col_out, col_in, 0, east_id),
            (col_out, col_in, 1, west_id),
        )
    ):
        edges.append(
            pltpu.make_async_remote_copy(
                src_ref=source.at[side],
                dst_ref=sink.at[side],
                send_sem=edge_send.at[e],
                recv_sem=edge_recv.at[e],
                device_id=there,
                device_id_type=MESH,
            )
        )
        edges[-1].start()
    for b in range(16):
        rows = pl.ds(b * HALF, HALF)
        value = energy[rows, :]
        west = jnp.where(lane_h % TILE == 0, 0.0, pltpu.roll(value, 1, 1))
        east = jnp.where(lane_h % TILE == TILE - 1, 0.0, pltpu.roll(value, 127, 1))
        south = jnp.where(lane_h < TILE, 0.0, pltpu.roll(value, TILE, 1))
        north = jnp.where(lane_h >= 112, 0.0, pltpu.roll(value, 112, 1))
        e, n = east_wide[rows, :], north_wide[rows, :]
        result = (1.0 - jnp.abs(e) - jnp.abs(n)) * value + jnp.maximum(e, 0.0) * west
        result = result + jnp.maximum(-e, 0.0) * east
        result = result + jnp.maximum(n, 0.0) * south
        moved[rows, :] = result + jnp.maximum(-n, 0.0) * north

    for edge in edges:
        edge.wait()

    has_south = jnp.logical_or(slab > 0, z > 0)
    has_north = jnp.logical_or(slab < 3, z < 15)
    keep_south = jnp.where(has_south, 1.0, 0.0)
    keep_north = jnp.where(has_north, 1.0, 0.0)
    for b in range(16):
        g, u = b // 2, b % 2
        rows = pl.ds(b * HALF, HALF)
        packed = pl.ds(u * HALF, HALF)
        west, east = col_in[0], col_in[1]
        west = pltpu.roll(west, 128 - b, 1) if b else west
        east = pltpu.roll(east, 15 - b, 1) if b != 15 else east
        south = keep_south * row_in[0, packed, :]
        south = pltpu.roll(south, 128 - TILE * g, 1) if g else south
        north = keep_north * row_in[1, packed, :]
        north = pltpu.roll(north, 112 - TILE * g, 1) if g < 7 else north
        e, n = east_wide[rows, :], north_wide[rows, :]
        result = moved[rows, :]
        result = result + jnp.where(lane_h % TILE == 0, jnp.maximum(e, 0.0) * west, 0.0)
        result = result + jnp.where(lane_h % TILE == TILE - 1, jnp.maximum(-e, 0.0) * east, 0.0)
        result = result + jnp.where(lane_h < TILE, jnp.maximum(n, 0.0) * south, 0.0)
        result = result + jnp.where(lane_h >= 112, jnp.maximum(-n, 0.0) * north, 0.0)
        moved[rows, :] = result
        if u:
            both = pl.ds(g * GROUP, GROUP)
            result = moved[both, :]
            rounded[both, :] = result.astype(jnp.bfloat16)
            square[both, :] = (result * result).astype(jnp.bfloat16)
    for j in range(OWN):
        outbox2[pl.ds(j, WIDE, stride=PAD), :] = interact(pl.ds(j * WIDE, WIDE))

    def send_back(pz, some):
        for base, _ in some:
            peer = base + pz * 4
            pltpu.make_async_remote_copy(
                src_ref=outbox2.at[pl.ds(pl.multiple_of(peer * PAD, PAD), OWN)],
                dst_ref=inbox2.at[my_tile],
                send_sem=send_sem2,
                recv_sem=recv_sem2,
                device_id={"slab": slab, "wide": peer},
                device_id_type=MESH,
            ).start()

    def round_of(*tiers):
        def turns(turn, carry):
            pz = lax.rem(z + distance(turn), 16)
            for low, high, some, _ in tiers:

                @pl.when(jnp.logical_and(pz >= low, pz < high))
                def _(some=some):
                    send_back(pz, some)

            return carry

        lax.fori_loop(0, 15, turns, 0)
        for low, high, _, some in tiers:

            @pl.when(jnp.logical_and(z >= low, z < high))
            def _(some=some):
                send_back(z, some)

    ahead, behind = places[:4], places[4:]
    round_of((0, FIRST, places, places[1:]), (FIRST, SECOND, ahead, ahead[1:]))
    round_of((FIRST, SECOND, behind, behind), (SECOND, 16, ahead, ahead[1:]))
    round_of((SECOND, 16, behind, behind))
    pltpu.make_async_copy(outbox2.at[mine], inbox2.at[my_tile], recv_sem2).start()
    pltpu.make_async_copy(spectrum, spectrum, recv_sem2).wait()

    for sem in (send_sem, send_sem2):
        most = plane.at[pl.ds(0, OWN - 1), pl.ds(0, ROWS)]
        pltpu.make_async_copy(most, most, sem).wait()
        rest = plane.at[0, pl.ds(0, ROWS - OWN)]
        pltpu.make_async_copy(rest, rest, sem).wait()


def unpack_kernel(results, out):
    block = lax.broadcasted_iota(jnp.int32, (8, 128), 1) // TILE

    def unpack(j, carry):
        for h in range(2):
            parts = [results[pl.ds(h * 128 + k * PAD + j, 8, stride=256), :] for k in range(8)]
            for k, part in enumerate(swap_blocks(parts, block)):
                out[j, pl.ds(8 * h + k, 8, stride=16), :] = part
        return carry

    lax.fori_loop(0, OWN, unpack, 0, unroll=3)


def body(spectrum, sea_mask, courant, slot_owner, coupling):
    vmem = pl.BlockSpec(memory_space=pltpu.VMEM)
    anywhere = pl.BlockSpec(memory_space=pltpu.HBM)
    f32, bf16, dma = jnp.float32, jnp.bfloat16, pltpu.SemaphoreType.DMA
    mailbox = pltpu.VMEM((WIDE * PAD, 128), f32)
    square_table = pltpu.VMEM((SLOTS, SLOTS), bf16)
    column = pltpu.VMEM((SLOTS, 128), f32)
    results = pl.pallas_call(
        kernel,
        out_shape=jax.ShapeDtypeStruct((WIDE * PAD, 128), f32),
        in_specs=[anywhere] * 5,
        out_specs=anywhere,
        scratch_shapes=[
            pltpu.VMEM((ROWS, 128), jnp.int32),
            pltpu.SMEM((1, NF), f32),
            pltpu.SMEM((OWN, 128), jnp.int32),
            pltpu.VMEM((OWN, 128), jnp.int32),
            pltpu.VMEM((16, 128), f32),
            pltpu.VMEM((5, 16, 128), f32),
            column,
            pltpu.VMEM((OWN, HOLD, 128), f32),
            square_table,
            mailbox,
            mailbox,
            mailbox,
            pltpu.VMEM((2, 16, 128), f32),
            pltpu.VMEM((2, 16, 128), f32),
            square_table,
            square_table,
            square_table,
            square_table,
            square_table,
            column,
            column,
            column,
            column,
            pltpu.VMEM((SLOTS, 128), bf16),
            pltpu.VMEM((SLOTS, 128), bf16),
            column,
            pltpu.VMEM((2, GROUP, 128), f32),
            pltpu.VMEM((2, GROUP, 128), f32),
            pltpu.VMEM((2, HALF, 128), f32),
            pltpu.VMEM((2, HALF, 128), f32),
            dma,
            dma,
            dma((3,)),
            dma,
            dma,
            dma,
            dma,
            dma,
            dma((2,)),
            dma((2,)),
            dma((4,)),
            dma((4,)),
        ],
        compiler_params=pltpu.CompilerParams(
            collective_id=0, has_side_effects=True, vmem_limit_bytes=60 << 20
        ),
    )(spectrum, sea_mask, courant.reshape(1, NF), slot_owner.reshape(OWN, 128), coupling)
    return pl.pallas_call(
        unpack_kernel,
        out_shape=jax.ShapeDtypeStruct((OWN, ROWS, 128), f32),
        in_specs=[vmem],
        out_specs=vmem,
        compiler_params=pltpu.CompilerParams(vmem_limit_bytes=16 << 20),
    )(results)


def solution(mesh):
    return jax.shard_map(
        body,
        mesh=mesh,
        in_specs=(P("wide", "slab", None), P("slab", None), P(), P(), P()),
        out_specs=P("wide", "slab", None),
        check_vma=False,
    )
```

```python
import math

import jax
import jax.numpy as jnp
from jax import lax
from jax.experimental import pallas as pl
from jax.experimental.pallas import tpu as pltpu
from jax.sharding import PartitionSpec as P

ND = 36
NF = 32
WIDE = 128
OWN = 9
PAD = 16
SLOTS = OWN * WIDE
ROWS = 128
HOLD = 144
TOP = 8
TILE = 16
GROUP = 144
HALF = 72
EARLY = 5
FIRST, SECOND = 3, 7
MESH = pl.DeviceIdType.MESH

time_step = 0.5


def place(me):
    return me // 64, (me // 4) % 16, me % 4


def tile_of(y, x):
    return jnp.where(y == 0, x, 7 - x)


def device_of(z, q):
    y = q // 4
    return y * 64 + z * 4 + jnp.where(y == 0, q, 7 - q)


def distance(turn):
    far = 8 - (turn + 1) // 2
    return lax.rem(jnp.where(lax.rem(turn, 2) == 1, far, 16 - far), 16)


def swap_blocks(parts, block):
    parts = list(parts)
    for bit in (4, 2, 1):
        high = (block & bit) != 0
        for a in range(8):
            if a & bit:
                continue
            first, second = parts[a], parts[a + bit]
            parts[a] = jnp.where(high, pltpu.roll(second, TILE * bit, 1), first)
            parts[a + bit] = jnp.where(high, second, pltpu.roll(first, 128 - TILE * bit, 1))
    return parts


def kernel(
    spectrum,
    sea_hbm,
    courant_hbm,
    owner_hbm,
    coupling,
    inbox2,
    sea_mask,
    courant,
    owner_scalar,
    owner_rows,
    owner,
    own_speed,
    natural,
    plane,
    table_in,
    outbox,
    inbox,
    outbox2,
    rim_out,
    rim_in,
    picker,
    picker_t,
    half_table,
    table,
    table_t,
    owner_wide,
    east_wide,
    north_wide,
    moved,
    rounded,
    square,
    energy,
    row_out,
    row_in,
    col_out,
    col_in,
    load_sem,
    sea_sem,
    small_sem,
    table_sem,
    send_sem,
    recv_sem,
    send_sem2,
    recv_sem2,
    rim_send,
    rim_recv,
    edge_send,
    edge_recv,
):
    slab = lax.axis_index("slab")
    me = lax.axis_index("wide")
    y, z, x = place(me)
    q = tile_of(y, x)
    spot = z * 8 + q
    places = []
    for p in range(8):
        py, px = lax.rem(y + p // 4, 2), lax.rem(x + p % 4, 4)
        places.append((py * 64 + px, tile_of(py, px)))
    up_slab, down_slab = (slab + 1) % 4, (slab + 3) % 4
    north_id = {
        "slab": jnp.where(z == 15, up_slab, slab),
        "wide": y * 64 + ((z + 1) % 16) * 4 + x,
    }
    south_id = {
        "slab": jnp.where(z == 0, down_slab, slab),
        "wide": y * 64 + ((z + 15) % 16) * 4 + x,
    }
    east_id = {"slab": slab, "wide": device_of(z, (q + 1) % 8)}
    west_id = {"slab": slab, "wide": device_of(z, (q + 7) % 8)}

    small_loads = [
        pltpu.make_async_copy(owner_hbm, owner_scalar, small_sem.at[0]),
        pltpu.make_async_copy(courant_hbm, courant, small_sem.at[1]),
        pltpu.make_async_copy(owner_hbm, owner_rows, small_sem.at[2]),
    ]
    sea_load = pltpu.make_async_copy(sea_hbm, sea_mask, sea_sem)
    for load in (*small_loads, sea_load):
        load.start()
    loads = pltpu.make_async_copy(spectrum, plane.at[:, pl.ds(TOP, ROWS)], load_sem)
    loads.start()
    table_load = pltpu.make_async_copy(coupling, table_in, table_sem)
    table_load.start()

    barrier = pltpu.get_barrier_semaphore()
    for there in (
        {"slab": up_slab, "wide": me},
        {"slab": down_slab, "wide": me},
        north_id,
        south_id,
    ):
        pl.semaphore_signal(barrier, inc=1, device_id=there, device_id_type=MESH)

    def greet(turn, first=0):
        pz = lax.rem(z + distance(turn), 16) if first == 0 else z
        for base, _ in places[first:]:
            pl.semaphore_signal(
                barrier, inc=1, device_id={"slab": slab, "wide": base + pz * 4}, device_id_type=MESH
            )

    for turn in (0, 1, 2, 3, 13, 14):
        greet(turn)
    greet(0, 1)
    for load in small_loads:
        load.wait()
    row16 = lax.broadcasted_iota(jnp.int32, (16, 128), 0)
    own_angle = jnp.zeros((16, 128), jnp.float32)
    own_courant = jnp.zeros((16, 128), jnp.float32)
    for j in range(OWN):
        slot = me * OWN + j
        component = owner_scalar[slot // 128, slot % 128]
        freq = component // ND
        angle = (component - freq * ND).astype(jnp.float32) * (2.0 * math.pi / ND)
        own_angle = jnp.where(row16 == j, angle, own_angle)
        own_courant = jnp.where(row16 == j, courant[0, freq], own_courant)
    east, north = own_courant * jnp.cos(own_angle), own_courant * jnp.sin(own_angle)
    own_speed[0] = 1.0 - jnp.abs(east) - jnp.abs(north)
    own_speed[1] = jnp.maximum(east, 0.0)
    own_speed[2] = jnp.maximum(-east, 0.0)
    own_speed[3] = jnp.maximum(north, 0.0)
    own_speed[4] = jnp.maximum(-north, 0.0)

    lane = lax.broadcasted_iota(jnp.int32, (8, 128), 1)
    block = lane // TILE

    sea_load.wait()
    loads.wait()
    sea = sea_mask[...].astype(jnp.float32)
    for j in range(OWN):
        plane[j, pl.ds(TOP, ROWS), :] = plane[j, pl.ds(TOP, ROWS), :] * sea
        plane[j, pl.ds(TOP - 8, 8), :] = jnp.zeros((8, 128), jnp.float32)
        plane[j, pl.ds(TOP + ROWS, 8), :] = jnp.zeros((8, 128), jnp.float32)
        rim_out[0, pl.ds(j, 1), :] = own_speed[3, pl.ds(j, 1), :] * plane[j, pl.ds(TOP + ROWS - 1, 1), :]
        rim_out[1, pl.ds(j, 1), :] = own_speed[4, pl.ds(j, 1), :] * plane[j, pl.ds(TOP, 1), :]

    def propagate(j, carry):
        greet(j + 4)
        remain, east, west, north, south = [own_speed[u, pl.ds(j, 1), :] for u in range(5)]
        for h in range(2):
            parts = []
            for k in range(8):
                start = TOP + 8 * h + k
                here = plane[j, pl.ds(start, 8, stride=16), :]
                part = remain * here + east * pltpu.roll(here, 1, 1)
                part = part + west * pltpu.roll(here, 127, 1)
                part = part + north * plane[j, pl.ds(start - 1, 8, stride=16), :]
                parts.append(part + south * plane[j, pl.ds(start + 1, 8, stride=16), :])
            for k, part in enumerate(swap_blocks(parts, block)):
                outbox[pl.ds(h * 128 + k * PAD + j, 8, stride=256), :] = part
        return carry

    lax.fori_loop(0, OWN, propagate, 0, unroll=3)

    pl.semaphore_wait(barrier, WIDE - 1 + 4)

    rims = []
    for side, there in ((0, up_slab), (1, down_slab)):
        rims.append(
            pltpu.make_async_remote_copy(
                src_ref=rim_out.at[side, pl.ds(0, OWN)],
                dst_ref=rim_in.at[side, pl.ds(0, OWN)],
                send_sem=rim_send.at[side],
                recv_sem=rim_recv.at[side],
                device_id={"slab": there, "wide": me},
                device_id_type=MESH,
            )
        )
        rims[-1].start()
    mine = pl.ds(pl.multiple_of(me * PAD, PAD), OWN)
    my_tile = pl.ds(pl.multiple_of(spot * PAD, PAD), OWN)

    def send(pz, first=0):
        for base, tile in places[first:]:
            pltpu.make_async_remote_copy(
                src_ref=outbox.at[pl.ds(pl.multiple_of((pz * 8 + tile) * PAD, PAD), OWN)],
                dst_ref=inbox.at[mine],
                send_sem=send_sem,
                recv_sem=recv_sem,
                device_id={"slab": slab, "wide": base + pz * 4},
                device_id_type=MESH,
            ).start()

    def send_inner(turn, carry):
        pz = lax.rem(z + distance(turn), 16)

        @pl.when(jnp.logical_and(pz > 0, pz < 15))
        def _():
            send(pz)

        return carry

    def send_outer(turn, carry):
        pz = lax.rem(z + distance(turn), 16)

        @pl.when(jnp.logical_or(pz == 0, pz == 15))
        def _():
            send(pz)

        return carry

    def send_any(turn, carry):
        send(lax.rem(z + distance(turn), 16))
        return carry

    lax.fori_loop(0, EARLY, send_inner, 0)
    for rim in rims:
        rim.wait()
    lane9 = lax.broadcasted_iota(jnp.int32, (OWN, 128), 1)
    below = jnp.where(slab > 0, 1.0, 0.0) * rim_in[0, pl.ds(0, OWN), :]
    above = jnp.where(slab < 3, 1.0, 0.0) * rim_in[1, pl.ds(0, OWN), :]
    for k in range(8):
        low = pltpu.roll(below, (128 - TILE * k) % 128, 1) if k else below
        rows = pl.ds(k * PAD, OWN)
        outbox[rows, :] = outbox[rows, :] + jnp.where(lane9 < TILE, low, 0.0)
        high = pltpu.roll(above, 112 - TILE * k, 1) if k < 7 else above
        rows = pl.ds((15 * 8 + k) * PAD, OWN)
        outbox[rows, :] = outbox[rows, :] + jnp.where(lane9 >= 112, high, 0.0)
    lax.fori_loop(0, EARLY, send_outer, 0)
    lax.fori_loop(EARLY, 15, send_any, 0)
    send(z, 1)
    pltpu.make_async_copy(outbox.at[my_tile], inbox.at[mine], recv_sem).start()

    owners = owner_rows[...].astype(jnp.float32)
    band = jnp.floor((owners + 0.5) * (1.0 / ND))
    angle = (owners - band * ND) * (2.0 * math.pi / ND)
    speed = jnp.zeros((OWN, 128), jnp.float32)
    for f in range(NF):
        speed = jnp.where(band == f, courant[0, f], speed)
    wide_rows = (owners, speed * jnp.cos(angle), speed * jnp.sin(angle))
    for wide_form, row_form in zip((owner_wide, east_wide, north_wide), wide_rows):
        for j in range(OWN):
            natural[pl.ds(j * 128, 128), :] = jnp.broadcast_to(row_form[j : j + 1], (128, 128)).T
        for j in range(OWN):
            wide_form[pl.ds(j * WIDE, WIDE), :] = natural[pl.ds(j, WIDE, stride=OWN), :]
    for j in range(OWN):
        owner[pl.ds(j, 1), :] = owner_wide[pl.ds(j * WIDE, WIDE), :].T[0:1]

    lanes = lax.broadcasted_iota(jnp.int32, (128, 128), 1).astype(jnp.float32)
    sublanes = lax.broadcasted_iota(jnp.int32, (128, 128), 0).astype(jnp.float32)

    def pick(i, carry):
        rows = pl.ds(pl.multiple_of(i * 128, 128), 128)
        base = (i * 128).astype(jnp.float32)
        for j in range(OWN):
            columns = pl.ds(j * 128, 128)
            hit = owner_wide[rows, :] == lanes + 128.0 * j
            picker[rows, columns] = jnp.where(hit, 1.0, 0.0).astype(jnp.bfloat16)
            hit = owner[pl.ds(j, 1), :] == sublanes + base
            picker_t[rows, columns] = jnp.where(hit, 1.0, 0.0).astype(jnp.bfloat16)
        return carry

    lax.fori_loop(0, OWN, pick, 0)
    table_load.wait()

    def rows_picked(i, carry):
        rows = pl.ds(pl.multiple_of(i * 128, 128), 128)
        half_table[rows, :] = jnp.dot(
            picker[rows, :], table_in[...], preferred_element_type=jnp.float32
        ).astype(jnp.bfloat16)
        return carry

    lax.fori_loop(0, OWN, rows_picked, 0)

    def columns_picked(i, carry):
        rows = pl.ds(pl.multiple_of(i * 128, 128), 128)
        full = jnp.dot(half_table[rows, :], picker_t[...], preferred_element_type=jnp.float32)
        table[rows, :] = full.astype(jnp.bfloat16)
        for j in range(OWN):
            table_t[pl.ds(j * 128, 128), rows] = full[:, j * 128 : (j + 1) * 128].T.astype(jnp.bfloat16)
        return carry

    lax.fori_loop(0, OWN, columns_picked, 0)

    tile_sea = sea_mask[pl.ds(pl.multiple_of(z * 8, 8), 8), :].astype(jnp.float32)
    column = lax.broadcasted_iota(jnp.int32, (128, 128), 0)
    target = lax.broadcasted_iota(jnp.int32, (128, 128), 1)
    spread = jnp.where(column == q * TILE + target % TILE, 1.0, 0.0)
    tile_sea = jnp.dot(tile_sea, spread, preferred_element_type=jnp.float32)
    inner = lax.broadcasted_iota(jnp.int32, (8, 128), 0)
    tile_sea = jnp.sum(jnp.where(inner == block, tile_sea, 0.0), axis=0, keepdims=True)

    pltpu.make_async_copy(spectrum, spectrum, recv_sem).wait()
    for j in range(OWN):
        rows = pl.ds(j * WIDE, WIDE)
        value = inbox[pl.ds(j, WIDE, stride=PAD), :]
        moved[rows, :] = value
        rounded[rows, :] = value.astype(jnp.bfloat16)
        square[rows, :] = (value * value).astype(jnp.bfloat16)

    def interact(rows):
        value = moved[rows, :]
        gain = value * jnp.dot(table[rows, :], rounded[...], preferred_element_type=jnp.float32)
        loss = jnp.dot(table_t[rows, :], square[...], preferred_element_type=jnp.float32)
        return tile_sea * jnp.maximum(value + time_step * (gain - loss), 0.0)

    lane_g = lax.broadcasted_iota(jnp.int32, (GROUP, 128), 1)
    lane_h = lax.broadcasted_iota(jnp.int32, (HALF, 128), 1)
    for g in range(8):
        rows = pl.ds(g * GROUP, GROUP)
        value = interact(rows)
        energy[rows, :] = value
        north = pltpu.roll(value, (TILE * (g + 1)) % 128, 1) if g < 7 else value
        south = pltpu.roll(value, TILE * g, 1) if g else value
        here = lane_g // TILE == g
        if g:
            north = jnp.where(here, north, row_out[0])
            south = jnp.where(here, south, row_out[1])
        row_out[0] = north
        row_out[1] = south
        for u in range(2):
            b = 2 * g + u
            part = value[u * HALF : (u + 1) * HALF]
            east = pltpu.roll(part, (b + 113) % 128, 1) if b != 15 else part
            west = pltpu.roll(part, b, 1) if b else part
            here = lane_h % TILE == b
            if b:
                east = jnp.where(here, east, col_out[0])
                west = jnp.where(here, west, col_out[1])
            col_out[0] = east
            col_out[1] = west

    edges = []
    for e, (source, sink, side, there) in enumerate(
        (
            (row_out, row_in, 0, north_id),
            (row_out, row_in, 1, south_id),
            (col_out, col_in, 0, east_id),
            (col_out, col_in, 1, west_id),
        )
    ):
        edges.append(
            pltpu.make_async_remote_copy(
                src_ref=source.at[side],
                dst_ref=sink.at[side],
                send_sem=edge_send.at[e],
                recv_sem=edge_recv.at[e],
                device_id=there,
                device_id_type=MESH,
            )
        )
        edges[-1].start()
    for b in range(16):
        rows = pl.ds(b * HALF, HALF)
        value = energy[rows, :]
        west = jnp.where(lane_h % TILE == 0, 0.0, pltpu.roll(value, 1, 1))
        east = jnp.where(lane_h % TILE == TILE - 1, 0.0, pltpu.roll(value, 127, 1))
        south = jnp.where(lane_h < TILE, 0.0, pltpu.roll(value, TILE, 1))
        north = jnp.where(lane_h >= 112, 0.0, pltpu.roll(value, 112, 1))
        e, n = east_wide[rows, :], north_wide[rows, :]
        result = (1.0 - jnp.abs(e) - jnp.abs(n)) * value + jnp.maximum(e, 0.0) * west
        result = result + jnp.maximum(-e, 0.0) * east
        result = result + jnp.maximum(n, 0.0) * south
        moved[rows, :] = result + jnp.maximum(-n, 0.0) * north

    for edge in edges:
        edge.wait()

    has_south = jnp.logical_or(slab > 0, z > 0)
    has_north = jnp.logical_or(slab < 3, z < 15)
    keep_south = jnp.where(has_south, 1.0, 0.0)
    keep_north = jnp.where(has_north, 1.0, 0.0)
    for b in range(16):
        g, u = b // 2, b % 2
        rows = pl.ds(b * HALF, HALF)
        packed = pl.ds(u * HALF, HALF)
        west, east = col_in[0], col_in[1]
        west = pltpu.roll(west, 128 - b, 1) if b else west
        east = pltpu.roll(east, 15 - b, 1) if b != 15 else east
        south = keep_south * row_in[0, packed, :]
        south = pltpu.roll(south, 128 - TILE * g, 1) if g else south
        north = keep_north * row_in[1, packed, :]
        north = pltpu.roll(north, 112 - TILE * g, 1) if g < 7 else north
        e, n = east_wide[rows, :], north_wide[rows, :]
        result = moved[rows, :]
        result = result + jnp.where(lane_h % TILE == 0, jnp.maximum(e, 0.0) * west, 0.0)
        result = result + jnp.where(lane_h % TILE == TILE - 1, jnp.maximum(-e, 0.0) * east, 0.0)
        result = result + jnp.where(lane_h < TILE, jnp.maximum(n, 0.0) * south, 0.0)
        result = result + jnp.where(lane_h >= 112, jnp.maximum(-n, 0.0) * north, 0.0)
        moved[rows, :] = result
        if u:
            both = pl.ds(g * GROUP, GROUP)
            result = moved[both, :]
            rounded[both, :] = result.astype(jnp.bfloat16)
            square[both, :] = (result * result).astype(jnp.bfloat16)
    for j in range(OWN):
        outbox2[pl.ds(j, WIDE, stride=PAD), :] = interact(pl.ds(j * WIDE, WIDE))

    def send_back(pz, some):
        for base, _ in some:
            peer = base + pz * 4
            pltpu.make_async_remote_copy(
                src_ref=outbox2.at[pl.ds(pl.multiple_of(peer * PAD, PAD), OWN)],
                dst_ref=inbox2.at[my_tile],
                send_sem=send_sem2,
                recv_sem=recv_sem2,
                device_id={"slab": slab, "wide": peer},
                device_id_type=MESH,
            ).start()

    def round_of(*tiers):
        def turns(turn, carry):
            pz = lax.rem(z + distance(turn), 16)
            for low, high, some, _ in tiers:

                @pl.when(jnp.logical_and(pz >= low, pz < high))
                def _(some=some):
                    send_back(pz, some)

            return carry

        lax.fori_loop(0, 15, turns, 0)
        for low, high, _, some in tiers:

            @pl.when(jnp.logical_and(z >= low, z < high))
            def _(some=some):
                send_back(z, some)

    ahead, behind = places[:4], places[4:]
    round_of((0, FIRST, places, places[1:]), (FIRST, SECOND, ahead, ahead[1:]))
    round_of((FIRST, SECOND, behind, behind), (SECOND, 16, ahead, ahead[1:]))
    round_of((SECOND, 16, behind, behind))
    pltpu.make_async_copy(outbox2.at[mine], inbox2.at[my_tile], recv_sem2).start()
    pltpu.make_async_copy(spectrum, spectrum, recv_sem2).wait()

    for sem in (send_sem, send_sem2):
        most = plane.at[pl.ds(0, OWN - 1), pl.ds(0, ROWS)]
        pltpu.make_async_copy(most, most, sem).wait()
        rest = plane.at[0, pl.ds(0, ROWS - OWN)]
        pltpu.make_async_copy(rest, rest, sem).wait()


def unpack_kernel(results, out):
    block = lax.broadcasted_iota(jnp.int32, (8, 128), 1) // TILE

    def unpack(j, carry):
        for h in range(2):
            parts = [results[pl.ds(h * 128 + k * PAD + j, 8, stride=256), :] for k in range(8)]
            for k, part in enumerate(swap_blocks(parts, block)):
                out[j, pl.ds(8 * h + k, 8, stride=16), :] = part
        return carry

    lax.fori_loop(0, OWN, unpack, 0, unroll=3)


def body(spectrum, sea_mask, courant, slot_owner, coupling):
    vmem = pl.BlockSpec(memory_space=pltpu.VMEM)
    anywhere = pl.BlockSpec(memory_space=pltpu.HBM)
    f32, bf16, dma = jnp.float32, jnp.bfloat16, pltpu.SemaphoreType.DMA
    mailbox = pltpu.VMEM((WIDE * PAD, 128), f32)
    square_table = pltpu.VMEM((SLOTS, SLOTS), bf16)
    column = pltpu.VMEM((SLOTS, 128), f32)
    results = pl.pallas_call(
        kernel,
        out_shape=jax.ShapeDtypeStruct((WIDE * PAD, 128), f32),
        in_specs=[anywhere] * 5,
        out_specs=anywhere,
        scratch_shapes=[
            pltpu.VMEM((ROWS, 128), jnp.int32),
            pltpu.SMEM((1, NF), f32),
            pltpu.SMEM((OWN, 128), jnp.int32),
            pltpu.VMEM((OWN, 128), jnp.int32),
            pltpu.VMEM((16, 128), f32),
            pltpu.VMEM((5, 16, 128), f32),
            column,
            pltpu.VMEM((OWN, HOLD, 128), f32),
            square_table,
            mailbox,
            mailbox,
            mailbox,
            pltpu.VMEM((2, 16, 128), f32),
            pltpu.VMEM((2, 16, 128), f32),
            square_table,
            square_table,
            square_table,
            square_table,
            square_table,
            column,
            column,
            column,
            column,
            pltpu.VMEM((SLOTS, 128), bf16),
            pltpu.VMEM((SLOTS, 128), bf16),
            column,
            pltpu.VMEM((2, GROUP, 128), f32),
            pltpu.VMEM((2, GROUP, 128), f32),
            pltpu.VMEM((2, HALF, 128), f32),
            pltpu.VMEM((2, HALF, 128), f32),
            dma,
            dma,
            dma((3,)),
            dma,
            dma,
            dma,
            dma,
            dma,
            dma((2,)),
            dma((2,)),
            dma((4,)),
            dma((4,)),
        ],
        compiler_params=pltpu.CompilerParams(
            collective_id=0, has_side_effects=True, vmem_limit_bytes=60 << 20
        ),
    )(spectrum, sea_mask, courant.reshape(1, NF), slot_owner.reshape(OWN, 128), coupling)
    return pl.pallas_call(
        unpack_kernel,
        out_shape=jax.ShapeDtypeStruct((OWN, ROWS, 128), f32),
        in_specs=[vmem],
        out_specs=vmem,
        compiler_params=pltpu.CompilerParams(vmem_limit_bytes=16 << 20),
    )(results)


def solution(mesh):
    return jax.shard_map(
        body,
        mesh=mesh,
        in_specs=(P("wide", "slab", None), P("slab", None), P(), P(), P()),
        out_specs=P("wide", "slab", None),
        check_vma=False,
    )
```
